32 devices in a mesh: fsdp: 32 (over z, y, x, core).
Axes of the slice: x: 2, y: 2, z: 4, core: 2. Of those that a mesh axis runs over, the one named last changes fastest.
Arguments:
- tokens: bfloat16 [32768, 768], P('fsdp'), may hold values from -6 to 6
- cotangent: bfloat16 [32768, 768], P('fsdp'), may hold values from -6 to 6
- lengths: int32 [32, 4], P('fsdp'), may hold values from 0 to 1024, as said below
- routes: int32 [32768, 1], P('fsdp'), may hold values from 0 to 3; in each aligned block of 1024 rows (0 to 1023, 1024 to 2047, ...) at most 512 rows name the same one
- gain_attn: bfloat16 [768], P('fsdp'), may hold values from 0.5 to 1.5
- w_qkv: bfloat16 [768, 2304], P('fsdp'), may hold values from -0.21875 to 0.21875
- w_out: bfloat16 [768, 768], P('fsdp'), may hold values from -1.75 to 1.75
- table: bfloat16 [32, 12], replicated, may hold values from -4 to 4
- gain_ffn: bfloat16 [768], P('fsdp'), may hold values from 0.5 to 1.5
- router: bfloat16 [768, 4], P('fsdp'), may hold values from -0.21875 to 0.21875
- expert_up: bfloat16 [3072, 4, 768], P('fsdp'), may hold values from -0.21875 to 0.21875
- expert_down: bfloat16 [3072, 4, 768], P('fsdp'), may hold values from -0.4375 to 0.4375
Outputs:
- output: bfloat16 [32768, 768], P('fsdp')
- grad_tokens: bfloat16 [32768, 768], P('fsdp')
- grad_gain_attn: float32 [768], P('fsdp')
- grad_w_qkv: float32 [768, 2304], P('fsdp')
- grad_w_out: float32 [768, 768], P('fsdp')
- grad_table: float32 [32, 12], replicated
- grad_gain_ffn: float32 [768], P('fsdp')
- grad_router: float32 [768, 4], P('fsdp')
- grad_up: float32 [3072, 4, 768], P('fsdp')
- grad_down: float32 [3072, 4, 768], P('fsdp')
The draws below stay inside these ranges and needn't reach their ends.
Inputs may be any that keep to these rules, and one draw needn't show every extreme that they name: `lengths`: each row sums to 1024; some row is one sequence of 1024 tokens. `routes`: among the 1024 rows of one device no expert is named more than 512 times, a bound that some block reaches.
All inputs are finite; a program needn't handle non-finite values.
Results may differ from the reference program's by a relative error of at most 0.015.
Values may be sent and summed in bfloat16 or wider, within the bound.
No kernel may reach another device: no remote copies, remote signals or barrier semaphores. Data moves between devices by JAX's collectives and lax.ppermute only.
A program may use at most 448 MiB of HBM per device.

```python
import math
from functools import partial
import jax
import jax.numpy as jnp
import numpy as np
from jax import lax

D = 768
HEADS = 12
HEAD_DIM = 64
FF = 3072
BUCKETS = 32
EXPERTS = 4
DOCS = 4
TOK_DEV = 1024
CAP = 512
TOKENS = 32768
N_FSDP = 32


def draw_lengths(key, part):
    key = jax.random.fold_in(key, 11)
    cut_key, pick_key = jax.random.split(key)
    cuts = jnp.sort(jax.random.randint(cut_key, (N_FSDP, DOCS - 1), 0, TOK_DEV + 1), axis=1)
    edges = jnp.concatenate([jnp.zeros((N_FSDP, 1), jnp.int32), cuts.astype(jnp.int32), jnp.full((N_FSDP, 1), TOK_DEV, jnp.int32)], axis=1)
    pieces = edges[:, 1:] - edges[:, :-1]
    whole_row = jax.random.randint(pick_key, (), 0, N_FSDP)
    single = (lax.iota(jnp.int32, DOCS) == 0).astype(jnp.int32) * TOK_DEV
    picked = (lax.iota(jnp.int32, N_FSDP) == whole_row)[:, None]
    return jnp.where(picked, single[None, :], pieces).astype(jnp.int32)


def level_of(key, shape, cuts, low, top_value):
    level, own = 1.0, jax.random.fold_in(key, 6)
    for axis_at, blocks in cuts:
        draws = jnp.exp(jax.random.uniform(jax.random.fold_in(own, axis_at), (blocks,), jnp.float32, low / len(cuts), top_value / len(cuts)))
        level = level * jnp.repeat(draws, shape[axis_at] // blocks).reshape([-1 if axis == axis_at else 1 for axis in range(len(shape))])
    return level


def deal_out(own_key, own, number, rows, amount, top, reach, lean):
    ranking = jax.random.permutation(own_key, amount)
    heavy_load, usual = shares(amount, rows * top, reach, lean, True), shares(amount, rows * top, reach, lean, False)
    places = jnp.arange(amount)

    def named(sizes, offset_by):
        used = int((sizes > 0).sum())
        fixed = max(1, used // 4)
        passed = fixed + (places - fixed + offset_by * (used - fixed)) % max(1, amount - fixed)
        return jnp.zeros((amount,), jnp.int32).at[ranking[jnp.where(places < fixed, places, passed)]].set(jnp.asarray(sizes, jnp.int32))

    sizes = jnp.where(number % 4 == 0, named(heavy_load, number // 4), named(usual, number - number // 4 - 1))
    mixed = jax.random.permutation(jax.random.fold_in(own, 3), amount)
    donor, taker = mixed[0:amount // 2 * 2:2], mixed[1:amount // 2 * 2:2]
    slack = jnp.minimum(sizes[donor] - 1, reach - sizes[taker]) // 2
    slack = jnp.where((donor == ranking[0]) | (taker == ranking[0]) | (sizes[taker] == 0), 0, jnp.maximum(slack, 0))
    passed = jax.random.randint(jax.random.fold_in(own, 4), (amount // 2,), 0, 1 << 20) % (slack + 1)
    sizes = sizes.at[donor].add(-passed).at[taker].add(passed)
    labels = jnp.searchsorted(jnp.cumsum(sizes), jnp.arange(rows * top), side="right").astype(jnp.int32)
    grid = labels.reshape(top, rows).T
    grid = grid[jax.random.permutation(jax.random.fold_in(own, 1), rows)]
    offset_by = jax.random.randint(jax.random.fold_in(own, 2), (rows, 1), 0, top)
    return jnp.take_along_axis(grid, (jnp.arange(top)[None, :] + offset_by) % top, axis=1)


def shares(count, total, limit, skew, full):
    loads = [(1 << 20) // math.isqrt(rank ** skew) + 1 for rank in range(1, count + 1)]
    largest = limit if full else min(limit, max(-(-total // count), total * loads[0] // sum(loads)))
    least = 1 if total - largest >= count - 1 else 0
    given, rest = [largest] + [least] * (count - 1), total - largest - least * (count - 1)
    while rest > 0:
        movable = [i for i in range(1, count) if given[i] < largest] or [i for i in range(1, count) if given[i] < limit]
        pool, remaining = sum([loads[i] for i in movable]), rest
        for i in movable:
            more = min(limit - given[i], max(1, remaining * loads[i] // pool), rest)
            given[i] = given[i] + more
            rest = rest - more
    return np.array(given)


def normal_values(key, shape, spread, reach, cuts=(), kind=jnp.bfloat16):
    values = jax.random.normal(key, shape, jnp.float32) * spread
    if len(cuts) > 0:
        values = level_of(key, shape, cuts, -0.22, 0.18) * values
    return jnp.clip(values, min=-reach, max=reach).astype(kind)


def setup_inputs(seed: int = 0) -> dict:
    key_list = jax.random.split(jax.random.key(seed), 13)
    tokens = normal_values(key_list[0], (TOKENS, D), 1.0, 6.0, ((0, 32),))
    cotangent = normal_values(key_list[1], (TOKENS, D), 1.0, 6.0, ((0, 32),))
    lengths = draw_lengths(jax.random.fold_in(key_list[12], 71), 0)
    routes_keys = jax.random.split(jax.random.fold_in(key_list[3], 1), TOKENS // TOK_DEV)
    routes_turns = jax.random.permutation(jax.random.fold_in(key_list[3], 3), TOKENS // TOK_DEV)
    routes = jax.vmap(lambda own, number: deal_out(jax.random.fold_in(key_list[3], 2), own, number, TOK_DEV, EXPERTS, 1, CAP, 2))(routes_keys, routes_turns).reshape((TOKENS, 1))
    gain_attn = jnp.clip(1.0 + 0.1 * jax.random.normal(key_list[4], (D,), jnp.float32), 0.5, 1.5).astype(jnp.bfloat16)
    w_qkv = normal_values(key_list[5], (D, 3 * D), D ** -0.5, 0.21875, ((0, 32),))
    w_out = normal_values(key_list[6], (D, D), (D // 64) ** -0.5, 1.75, ((0, 32),))
    table = normal_values(key_list[7], (BUCKETS, HEADS), 1.0, 4.0)
    gain_ffn = jnp.clip(1.0 + 0.1 * jax.random.normal(key_list[8], (D,), jnp.float32), 0.5, 1.5).astype(jnp.bfloat16)
    router = normal_values(key_list[9], (D, EXPERTS), D ** -0.5, 0.21875, ((0, 32),))
    expert_up = normal_values(key_list[10], (FF, EXPERTS, D), D ** -0.5, 0.21875, ((0, 32),))
    expert_down = normal_values(key_list[11], (FF, EXPERTS, D), (FF // 16) ** -0.5, 0.4375, ((0, 32),))
    return {"tokens": tokens, "cotangent": cotangent, "lengths": lengths, "routes": routes, "gain_attn": gain_attn, "w_qkv": w_qkv, "w_out": w_out, "table": table, "gain_ffn": gain_ffn, "router": router, "expert_up": expert_up, "expert_down": expert_down}


@jax.custom_vjp
def low(v):
    return lax.optimization_barrier(v.astype(jnp.bfloat16)).astype(jnp.float32)

@jax.custom_vjp
def low_back(v):
    return v

def low_keep(v):
    return (low(v), None)

def low_pass(kept, grad):
    return (grad,)

def back_keep(v):
    return (v, None)

def back_low(kept, grad):
    return (low(grad),)
low.defvjp(low_keep, low_pass)
low_back.defvjp(back_keep, back_low)
highest = lax.Precision.HIGHEST
norm_eps = 1e-06
masked_fill = -1e+30
far_steps = (12, 16, 23, 32, 46, 64, 91)

def bucket_of(offset):
    distance = jnp.abs(offset)
    far_bucket = 8 + sum(((distance >= step).astype(jnp.int32) for step in far_steps))
    return jnp.where(distance < 8, distance, far_bucket) + 16 * (offset > 0).astype(jnp.int32)

def rms_norm(values, gain):
    return values * lax.rsqrt(lax.optimization_barrier(jnp.mean(values * values, axis=-1, keepdims=True)) + norm_eps) * gain

def attend(table, packed):
    qkv_rows, doc_ids = packed
    queries = qkv_rows[:, :D].reshape(TOK_DEV, HEADS, HEAD_DIM)
    key_rows = qkv_rows[:, D:2 * D].reshape(TOK_DEV, HEADS, HEAD_DIM)
    value_rows = qkv_rows[:, 2 * D:].reshape(TOK_DEV, HEADS, HEAD_DIM)
    places = lax.iota(jnp.int32, TOK_DEV)
    buckets = bucket_of(places[None, :] - places[:, None])
    bias = jnp.transpose(table[buckets], (2, 0, 1))
    raw = jnp.einsum('qhd,khd->hqk', queries, key_rows, precision=highest) * 0.125
    scores = low_back(raw + bias)
    same_doc = doc_ids[:, None] == doc_ids[None, :]
    masked = jnp.where(same_doc[None], scores, masked_fill)
    top = lax.optimization_barrier(jnp.max(masked, axis=-1, keepdims=True))
    expo = jnp.exp(masked - top)
    probs = low(expo / lax.optimization_barrier(jnp.sum(expo, axis=-1, keepdims=True)))
    mixed = jnp.einsum('hqk,khd->qhd', probs, value_rows, precision=highest).reshape(TOK_DEV, D)
    return low(low_back(mixed))

def expert_apply(packed):
    rows, up_one, down_one = packed
    pre_act = low_back(jnp.dot(rows, up_one.T, precision=highest))
    hidden = low(jax.nn.gelu(pre_act))
    return low_back(jnp.dot(hidden, down_one, precision=highest))

def layer(tokens_f, gain_attn, w_qkv, w_out, table, gain_ffn, router, expert_up, expert_down, doc_ids, flat_slot, route_hot):
    normed = low(rms_norm(tokens_f, gain_attn))
    qkv_rows = low(low_back(jnp.dot(normed, w_qkv, precision=highest)))
    mixed = lax.map(jax.checkpoint(partial(attend, table)), (qkv_rows.reshape(N_FSDP, TOK_DEV, 3 * D), doc_ids))
    attn_out = low_back(jnp.dot(mixed.reshape(TOKENS, D), w_out, precision=highest))
    attended = tokens_f + attn_out
    normed_ffn = low(rms_norm(attended, gain_ffn))
    logits = low_back(jnp.dot(normed_ffn, router, precision=highest))
    gate_value = lax.optimization_barrier(jnp.sum(jax.nn.softmax(logits, axis=-1) * route_hot, axis=-1, keepdims=True))
    dispatched = jnp.zeros((N_FSDP * EXPERTS * CAP, D), jnp.float32).at[flat_slot].set(normed_ffn)
    dispatched = jnp.transpose(dispatched.reshape(N_FSDP, EXPERTS, CAP, D), (1, 0, 2, 3)).reshape(EXPERTS, N_FSDP * CAP, D)
    expert_rows = lax.map(jax.checkpoint(expert_apply), (dispatched, jnp.transpose(expert_up, (1, 0, 2)), jnp.transpose(expert_down, (1, 0, 2))))
    expert_rows = jnp.transpose(expert_rows.reshape(EXPERTS, N_FSDP, CAP, D), (1, 0, 2, 3)).reshape(N_FSDP * EXPERTS * CAP, D)
    return attended + gate_value * expert_rows[flat_slot]

def reference(tokens, cotangent, lengths, routes, gain_attn, w_qkv, w_out, table, gain_ffn, router, expert_up, expert_down):
    ends = jnp.cumsum(lengths, axis=1)
    places = lax.iota(jnp.int32, TOK_DEV)
    doc_ids = lax.optimization_barrier(jnp.sum((places[None, :, None] >= ends[:, None, :]).astype(jnp.int32), axis=2))
    route = routes[:, 0].reshape(N_FSDP, TOK_DEV)
    chosen = (route[:, :, None] == lax.iota(jnp.int32, EXPERTS)[None, None, :]).astype(jnp.int32)
    rank = lax.optimization_barrier(jnp.sum((jnp.cumsum(chosen, axis=1) - chosen) * chosen, axis=2))
    device_base = (lax.iota(jnp.int32, N_FSDP) * (EXPERTS * CAP))[:, None]
    flat_slot = (device_base + route * CAP + rank).reshape(TOKENS).astype(jnp.int32)
    route_hot = chosen.reshape(TOKENS, EXPERTS).astype(jnp.float32)
    floats = tuple((member.astype(jnp.float32) for member in (tokens, gain_attn, w_qkv, w_out, table, gain_ffn, router, expert_up, expert_down)))

    def forward(*inputs):
        return layer(*inputs, doc_ids, flat_slot, route_hot)
    output, pullback = jax.vjp(forward, *floats)
    grads = pullback(cotangent.astype(jnp.float32))
    return (output.astype(jnp.bfloat16), grads[0].astype(jnp.bfloat16), grads[1], grads[2], grads[3], grads[4], grads[5], grads[6], grads[7], grads[8])
```

```python
import functools

import jax
import jax.numpy as jnp
from jax import lax
from jax.experimental import pallas as pl
from jax.experimental.pallas import tpu as pltpu
from jax.sharding import PartitionSpec as P

D = 768
HEADS = 12
HEAD_DIM = 64
PAIRS = HEADS // 2
BUCKETS = 32
EXPERTS = 4
TOK_DEV = 1024
CAP = 512
ROWS = EXPERTS * CAP
AXIS = "fsdp"
F32 = jnp.float32
BF16 = jnp.bfloat16

norm_eps = 1e-06
masked_fill = -1e30
far_steps = (12, 16, 23, 32, 46, 64, 91)

TILE = 128
KEY_TILES = TOK_DEV // TILE
QUERY_BLOCK = 256
QUERY_BLOCKS = TOK_DEV // QUERY_BLOCK
HALVES = QUERY_BLOCK // TILE
NT = (((1,), (1,)), ((), ()))
NN = (((1,), (0,)), ((), ()))
TN = (((0,), (0,)), ((), ()))


def bucket_of(offset):
    distance = jnp.abs(offset)
    far_bucket = 8 + sum(((distance >= step).astype(jnp.int32) for step in far_steps))
    return jnp.where(distance < 8, distance, far_bucket) + 16 * (offset > 0).astype(jnp.int32)


def rms_norm(values, gain):
    return values * lax.rsqrt(jnp.mean(values * values, axis=-1, keepdims=True) + norm_eps) * gain


def along_z(value, size, shift):
    depth = size // 8
    return lax.ppermute(
        value, AXIS, [(i, (i // 8 + shift) % depth * 8 + i % 8) for i in range(size)]
    )


def along_quad(value, size, flip):
    return lax.ppermute(value, AXIS, [(i, i ^ (flip << 1)) for i in range(size)])


def along_core(value, size):
    return lax.ppermute(value, AXIS, [(i, i ^ 1) for i in range(size)])


def scatter_sums(partial, size):
    me = lax.axis_index(AXIS)
    depth = size // 8
    z, quad, core = me // 8, me // 2 % 4, me % 2
    rows = partial.shape[0] // size
    view = partial.reshape(depth, 4, 2, rows, partial.shape[1])
    mine = lax.dynamic_index_in_dim(view, core, 2, False)
    other = lax.dynamic_index_in_dim(view, 1 - core, 2, False).astype(BF16)
    total = mine + along_core(other, size).astype(F32)
    low = total.astype(BF16)
    arrived = [
        along_quad(lax.dynamic_index_in_dim(low, quad ^ flip, 1, False), size, flip)
        for flip in range(1, 4)
    ]
    total = lax.dynamic_index_in_dim(total, quad, 1, False)
    for piece in arrived:
        total = total + piece.astype(F32)
    low = total.astype(BF16)
    arrived = [
        along_z(lax.dynamic_index_in_dim(low, (z + shift) % depth, 0, False), size, shift)
        for shift in range(1, depth)
    ]
    total = lax.dynamic_index_in_dim(total, z, 0, False)
    for piece in arrived:
        total = total + piece.astype(F32)
    return total


def sum_everywhere(value, size):
    step = 1
    while step < size:
        value = value + lax.ppermute(value, AXIS, [(i, i ^ step) for i in range(size)])
        step *= 2
    return value


def score_tile(tile, block, keys, queries, near_ref, head):
    scores = lax.dot_general(
        keys[tile * TILE : (tile + 1) * TILE], queries, NT, preferred_element_type=F32
    )
    parts = []
    for half in range(HALVES):
        part = scores[:, half * TILE : (half + 1) * TILE]
        apart = tile - (block * HALVES + half)
        if abs(apart) <= 1:
            part = part + near_ref[head, apart + 1]
        parts.append(part)
    return parts


def fold(value, combine):
    return combine(value.reshape(value.shape[0] // 8, 8, value.shape[1]), axis=0)


def attend_kernel(
    q_ref, k_ref, v_ref, extra_q_ref, extra_k_ref, near_ref, out_ref, log_ref,
    score_ref, prob_ref, turned_ref,
):
    lane = lax.broadcasted_iota(jnp.int32, (TOK_DEV, 2 * HEAD_DIM), 1)
    queries = (q_ref[...].astype(F32) * 0.125).astype(BF16)
    keys = k_ref[...]
    values_t = v_ref[...].astype(F32).T.astype(BF16)
    for head in range(2):
        own = (lane < HEAD_DIM) if head == 0 else (lane >= HEAD_DIM)
        head_keys = jnp.where(own, keys, extra_k_ref[head])
        head_queries = jnp.where(own, queries, extra_q_ref[head])
        head_values = values_t[head * HEAD_DIM : (head + 1) * HEAD_DIM]
        for block in range(QUERY_BLOCKS):
            side = block % 2
            at = slice(block * QUERY_BLOCK, (block + 1) * QUERY_BLOCK)
            top = None
            for tile in range(KEY_TILES):
                parts = score_tile(tile, block, head_keys, head_queries[at], near_ref, head)
                highs = []
                for half, part in enumerate(parts):
                    score_ref[
                        side, tile * TILE : (tile + 1) * TILE, half * TILE : (half + 1) * TILE
                    ] = part
                    highs.append(fold(part, jnp.max))
                high = jnp.concatenate(highs, axis=1)
                top = high if top is None else jnp.maximum(top, high)
            top = jnp.max(top, axis=0, keepdims=True)
            total = jnp.zeros((8, QUERY_BLOCK), F32)
            for tile in range(KEY_TILES):
                rows = slice(tile * TILE, (tile + 1) * TILE)
                expo = jnp.exp(score_ref[side, rows, :] - top)
                total = total + fold(expo, jnp.sum)
                prob_ref[side, rows, :] = expo.astype(BF16)
            total = jnp.sum(total, axis=0, keepdims=True)
            mixed = lax.dot_general(head_values, prob_ref[side], NN, preferred_element_type=F32)
            turned_ref[head * HEAD_DIM : (head + 1) * HEAD_DIM, at] = mixed * (1.0 / total)
            log_ref[0, head : head + 1, at] = top + jnp.log(total)
    out_ref[...] = turned_ref[...].T.astype(BF16)


def attend_back_kernel(
    q_ref, k_ref, v_ref, grad_ref, log_ref, extra_q_ref, extra_k_ref, near_ref, bucket_ref,
    grad_q_ref, grad_k_ref, grad_v_ref, grad_table_ref,
    prob_ref, slope_ref, low_prob_ref, low_grad_ref, turned_ref, key_sum_ref, value_sum_ref,
    near_sum_ref,
):
    lane = lax.broadcasted_iota(jnp.int32, (TOK_DEV, 2 * HEAD_DIM), 1)
    queries = (q_ref[...].astype(F32) * 0.125).astype(BF16)
    keys = k_ref[...]
    keys_t = (keys.astype(F32) * 0.125).T.astype(BF16)
    values = v_ref[...]
    grads = grad_ref[...]
    zero = jnp.zeros_like(grads)
    for head in range(2):
        own = (lane < HEAD_DIM) if head == 0 else (lane >= HEAD_DIM)
        head_keys = jnp.where(own, keys, extra_k_ref[head])
        head_queries = jnp.where(own, queries, extra_q_ref[head])
        bare_queries = jnp.where(own, queries, zero)
        head_grads = jnp.where(own, grads, zero)
        head_keys_t = keys_t[head * HEAD_DIM : (head + 1) * HEAD_DIM]
        near_sum_ref[...] = jnp.zeros_like(near_sum_ref)
        far_sums = [jnp.zeros((8, TILE), F32), jnp.zeros((8, TILE), F32)]
        for block in range(QUERY_BLOCKS):
            side = block % 2
            at = slice(block * QUERY_BLOCK, (block + 1) * QUERY_BLOCK)
            logs = log_ref[0, head : head + 1, at]
            delta = jnp.zeros((8, QUERY_BLOCK), F32)
            for tile in range(KEY_TILES):
                rows = slice(tile * TILE, (tile + 1) * TILE)
                parts = score_tile(tile, block, head_keys, head_queries[at], near_ref, head)
                probs = jnp.exp(jnp.concatenate(parts, axis=1) - logs)
                slopes = lax.dot_general(
                    values[rows], head_grads[at], NT, preferred_element_type=F32
                )
                delta = delta + fold(probs * slopes, jnp.sum)
                prob_ref[side, rows, :] = probs
                low_prob_ref[side, rows, :] = probs.astype(BF16)
                slope_ref[side, rows, :] = slopes
            delta = jnp.sum(delta, axis=0, keepdims=True)
            for tile in range(KEY_TILES):
                rows = slice(tile * TILE, (tile + 1) * TILE)
                grad_scores = prob_ref[side, rows, :] * (slope_ref[side, rows, :] - delta)
                low_grad_ref[side, rows, :] = grad_scores.astype(BF16)
                for half in range(HALVES):
                    part = grad_scores[:, half * TILE : (half + 1) * TILE]
                    apart = tile - (block * HALVES + half)
                    if abs(apart) <= 1:
                        near_sum_ref[apart + 1] += part
                    else:
                        which = 0 if apart < 0 else 1
                        far_sums[which] = far_sums[which] + fold(part, jnp.sum)
            value_part = lax.dot_general(
                low_prob_ref[side], head_grads[at], NN, preferred_element_type=F32
            )
            key_part = lax.dot_general(
                low_grad_ref[side], bare_queries[at], NN, preferred_element_type=F32
            )
            if head == 0 and block == 0:
                value_sum_ref[...] = value_part
                key_sum_ref[...] = key_part
            else:
                value_sum_ref[...] += value_part
                key_sum_ref[...] += key_part
            turned_ref[head * HEAD_DIM : (head + 1) * HEAD_DIM, at] = lax.dot_general(
                head_keys_t, low_grad_ref[side], NN, preferred_element_type=F32
            )
        for bucket in range(BUCKETS):
            row = jnp.zeros((8, TILE), F32)
            for apart in (-1, 0, 1):
                if (apart < 0 and bucket >= 16) or (apart > 0 and bucket < 16):
                    continue
                picked = jnp.where(
                    bucket_ref[apart + 1] == bucket, near_sum_ref[apart + 1], 0.0
                )
                row = row + fold(picked, jnp.sum)
            if bucket == 15:
                row = row + far_sums[0]
            if bucket == 31:
                row = row + far_sums[1]
            grad_table_ref[0, head, bucket : bucket + 1, :] = jnp.sum(row, axis=0, keepdims=True)
    grad_q_ref[...] = turned_ref[...].T.astype(BF16)
    grad_k_ref[...] = key_sum_ref[...].astype(BF16)
    grad_v_ref[...] = value_sum_ref[...].astype(BF16)


def column(first):
    return pl.BlockSpec((TOK_DEV, 2 * HEAD_DIM), lambda pair: (0, first + pair))


def score_specs():
    return [
        pl.BlockSpec((2, TOK_DEV, 2 * HEAD_DIM), lambda pair: (0, 0, 0)),
        pl.BlockSpec((2, TOK_DEV, 2 * HEAD_DIM), lambda pair: (pair, 0, 0)),
        pl.BlockSpec((2, 3, TILE, TILE), lambda pair: (pair, 0, 0, 0)),
    ]


def attend(qkv, extra_q, extra_k, near):
    logs = pl.BlockSpec((1, 2, TOK_DEV), lambda pair: (pair, 0, 0))
    return pl.pallas_call(
        attend_kernel,
        grid=(PAIRS,),
        in_specs=[column(0), column(PAIRS), column(2 * PAIRS)] + score_specs(),
        out_specs=[column(0), logs],
        out_shape=[
            jax.ShapeDtypeStruct((TOK_DEV, D), BF16),
            jax.ShapeDtypeStruct((PAIRS, 2, TOK_DEV), F32),
        ],
        scratch_shapes=[
            pltpu.VMEM((2, TOK_DEV, QUERY_BLOCK), F32),
            pltpu.VMEM((2, TOK_DEV, QUERY_BLOCK), BF16),
            pltpu.VMEM((2 * HEAD_DIM, TOK_DEV), F32),
        ],
        compiler_params=pltpu.CompilerParams(vmem_limit_bytes=40 << 20),
        cost_estimate=pl.CostEstimate(
            flops=40_000_000_000, bytes_accessed=12 << 20, transcendentals=HEADS << 20
        ),
    )(qkv, qkv, qkv, extra_q, extra_k, near)


def attend_back(qkv, grad_mixed, logs, extra_q, extra_k, near, buckets):
    log_spec = pl.BlockSpec((1, 2, TOK_DEV), lambda pair: (pair, 0, 0))
    return pl.pallas_call(
        attend_back_kernel,
        grid=(PAIRS,),
        in_specs=[column(0), column(PAIRS), column(2 * PAIRS), column(0), log_spec]
        + score_specs()
        + [pl.BlockSpec((3, TILE, TILE), lambda pair: (0, 0, 0))],
        out_specs=[
            column(0),
            column(0),
            column(0),
            pl.BlockSpec((1, 2, BUCKETS, TILE), lambda pair: (pair, 0, 0, 0)),
        ],
        out_shape=[
            jax.ShapeDtypeStruct((TOK_DEV, D), BF16),
            jax.ShapeDtypeStruct((TOK_DEV, D), BF16),
            jax.ShapeDtypeStruct((TOK_DEV, D), BF16),
            jax.ShapeDtypeStruct((PAIRS, 2, BUCKETS, TILE), F32),
        ],
        scratch_shapes=[
            pltpu.VMEM((2, TOK_DEV, QUERY_BLOCK), F32),
            pltpu.VMEM((2, TOK_DEV, QUERY_BLOCK), F32),
            pltpu.VMEM((2, TOK_DEV, QUERY_BLOCK), BF16),
            pltpu.VMEM((2, TOK_DEV, QUERY_BLOCK), BF16),
            pltpu.VMEM((2 * HEAD_DIM, TOK_DEV), F32),
            pltpu.VMEM((TOK_DEV, 2 * HEAD_DIM), F32),
            pltpu.VMEM((TOK_DEV, 2 * HEAD_DIM), F32),
            pltpu.VMEM((3, TILE, TILE), F32),
        ],
        compiler_params=pltpu.CompilerParams(vmem_limit_bytes=48 << 20),
        cost_estimate=pl.CostEstimate(
            flops=80_000_000_000, bytes_accessed=20 << 20, transcendentals=HEADS << 20
        ),
    )(qkv, qkv, qkv, grad_mixed, logs, extra_q, extra_k, near, buckets)


def score_extras(table, doc_ids):
    lane = lax.iota(jnp.int32, HEAD_DIM)
    places = lax.iota(jnp.int32, TOK_DEV)
    tiles = places // TILE
    is_doc = lane < 4
    block_lane = (lane >= 4) & (lane < 4 + KEY_TILES)
    same = doc_ids[:, None] == lane[None, :]
    in_block = tiles[:, None] == (lane - 4)[None, :]
    extra_q = jnp.where((is_doc & same) | (block_lane & in_block), 1.0, 0.0).astype(BF16)
    apart = tiles[:, None] - (lane - 4)[None, :]
    mask_k = jnp.where(is_doc & ~same, masked_fill, 0.0)
    far = jnp.where(
        apart[None] < 0, table[15].astype(F32)[:, None, None], table[31].astype(F32)[:, None, None]
    )
    use_far = (block_lane & (jnp.abs(apart) > 1))[None]
    extra_k = jnp.where(use_far, far, mask_k[None]).astype(BF16)
    blank = jnp.zeros_like(extra_q)
    queries = jnp.stack(
        [jnp.concatenate([blank, extra_q], axis=1), jnp.concatenate([extra_q, blank], axis=1)]
    )
    pairs = extra_k.reshape(PAIRS, 2, TOK_DEV, HEAD_DIM)
    even = jnp.concatenate([jnp.zeros_like(pairs[:, 0]), pairs[:, 0]], axis=-1)
    odd = jnp.concatenate([pairs[:, 1], jnp.zeros_like(pairs[:, 1])], axis=-1)
    keys = jnp.stack([even, odd], axis=1).reshape(HEADS, TOK_DEV, 2 * HEAD_DIM)
    return queries, keys


def gelu_with_slope(x):
    scale, cubic = 0.7978845608028654, 0.044715
    square = x * x
    curve = jnp.tanh(scale * x * (1.0 + cubic * square))
    half = 0.5 * (1.0 + curve)
    slope = half + 0.5 * x * (1.0 - curve * curve) * (scale * (1.0 + 3.0 * cubic * square))
    return x * half, slope


def expert_kernel(rows_ref, up_ref, down_ref, out_ref, hidden_ref, slope_ref, sum_ref):
    step = pl.program_id(0)
    up = up_ref[...].reshape(-1, D)
    down = down_ref[...].reshape(-1, D)
    for chunk in range(EXPERTS):
        at = slice(chunk * CAP, (chunk + 1) * CAP)
        pre = lax.dot_general(rows_ref[at], up, NT, preferred_element_type=F32)
        hidden, slope = gelu_with_slope(pre)
        low = hidden.astype(BF16)
        hidden_ref[at] = low
        slope_ref[at] = slope.astype(BF16)
        part = lax.dot_general(low, down, NN, preferred_element_type=F32)

        @pl.when(step == 0)
        def _():
            sum_ref[at] = part

        @pl.when(step > 0)
        def _():
            sum_ref[at] += part

    @pl.when(step == pl.num_programs(0) - 1)
    def _():
        out_ref[...] = sum_ref[...].astype(BF16)


def expert_back_kernel(grad_ref, slope_ref, up_ref, down_ref, out_ref, grad_pre_ref, sum_ref):
    step = pl.program_id(0)
    up = up_ref[...].reshape(-1, D)
    down = down_ref[...].reshape(-1, D)
    for chunk in range(EXPERTS):
        at = slice(chunk * CAP, (chunk + 1) * CAP)
        grad_hidden = lax.dot_general(grad_ref[at], down, NT, preferred_element_type=F32)
        grad_pre = (grad_hidden * slope_ref[at].astype(F32)).astype(BF16)
        grad_pre_ref[at] = grad_pre
        part = lax.dot_general(grad_pre, up, NN, preferred_element_type=F32)

        @pl.when(step == 0)
        def _():
            sum_ref[at] = part

        @pl.when(step > 0)
        def _():
            sum_ref[at] += part

    @pl.when(step == pl.num_programs(0) - 1)
    def _():
        out_ref[...] = sum_ref[...].astype(BF16)


def expert_weight_kernel(rows_ref, grad_ref, hidden_ref, grad_pre_ref, out_ref):
    pieces, _, units, _ = out_ref.shape
    grad_up = lax.dot_general(grad_pre_ref[...], rows_ref[...], TN, preferred_element_type=F32)
    out_ref[:, 0] = grad_up.astype(BF16).reshape(pieces, units, D)
    grad_down = lax.dot_general(hidden_ref[...], grad_ref[...], TN, preferred_element_type=F32)
    out_ref[:, 1] = grad_down.astype(BF16).reshape(pieces, units, D)


def expert_layout(weights):
    pieces, _, units, _ = weights.shape
    per_step = max(1, D // units)
    steps = pieces // per_step
    width = per_step * units
    whole = pl.BlockSpec((ROWS, D), lambda step: (0, 0))
    part = pl.BlockSpec((ROWS, width), lambda step: (0, step))
    up = pl.BlockSpec((per_step, 1, units, D), lambda step: (step, 0, 0, 0))
    down = pl.BlockSpec((per_step, 1, units, D), lambda step: (step, 1, 0, 0))
    both = pl.BlockSpec((per_step, 2, units, D), lambda step: (step, 0, 0, 0))
    return steps, width, whole, part, up, down, both


def expert_cost(products, total):
    return pl.CostEstimate(
        flops=products * 2 * ROWS * D * total, bytes_accessed=40 << 20, transcendentals=0
    )


def expert_forward(rows, weights):
    steps, width, whole, part, up, down, _ = expert_layout(weights)
    total = steps * width
    return pl.pallas_call(
        expert_kernel,
        grid=(steps,),
        in_specs=[whole, up, down],
        out_specs=[whole, part, part],
        out_shape=[
            jax.ShapeDtypeStruct((ROWS, D), BF16),
            jax.ShapeDtypeStruct((ROWS, total), BF16),
            jax.ShapeDtypeStruct((ROWS, total), BF16),
        ],
        scratch_shapes=[pltpu.VMEM((ROWS, D), F32)],
        compiler_params=pltpu.CompilerParams(vmem_limit_bytes=56 << 20),
        cost_estimate=expert_cost(2, total),
    )(rows, weights, weights)


def expert_backward(grad_rows, slopes, weights):
    steps, width, whole, part, up, down, _ = expert_layout(weights)
    total = steps * width
    return pl.pallas_call(
        expert_back_kernel,
        grid=(steps,),
        in_specs=[whole, part, up, down],
        out_specs=[whole, part],
        out_shape=[
            jax.ShapeDtypeStruct((ROWS, D), BF16),
            jax.ShapeDtypeStruct((ROWS, total), BF16),
        ],
        scratch_shapes=[pltpu.VMEM((ROWS, D), F32)],
        compiler_params=pltpu.CompilerParams(vmem_limit_bytes=56 << 20),
        cost_estimate=expert_cost(2, total),
    )(grad_rows, slopes, weights, weights)


def expert_weight_grads(rows, grad_rows, hidden, grad_pre, weights):
    steps, width, whole, part, _, _, both = expert_layout(weights)
    total = steps * width
    return pl.pallas_call(
        expert_weight_kernel,
        grid=(steps,),
        in_specs=[whole, whole, part, part],
        out_specs=both,
        out_shape=jax.ShapeDtypeStruct(weights.shape, BF16),
        compiler_params=pltpu.CompilerParams(vmem_limit_bytes=56 << 20),
        cost_estimate=expert_cost(2, total),
    )(rows, grad_rows, hidden, grad_pre)


def swap_rows(pieces, size):
    return [pieces[0]] + [along_quad(pieces[flip], size, flip) for flip in range(1, EXPERTS)]


def body(
    size,
    tokens,
    cotangent,
    lengths,
    routes,
    gain_attn,
    w_qkv,
    w_out,
    table,
    gain_ffn,
    router,
    expert_up,
    expert_down,
):
    quad = lax.axis_index(AXIS) // 2 % 4
    owned = w_qkv.shape[0]
    units = expert_up.shape[0]
    depth = size // 8
    same_expert = [
        [8 * z + 2 * q + c for z in range(depth) for c in range(2)] for q in range(EXPERTS)
    ]

    narrow = jnp.concatenate(
        [router, gain_attn[:, None], gain_ffn[:, None], jnp.zeros((owned, 128 - EXPERTS - 2), BF16)],
        axis=1,
    )
    dense = lax.all_gather(
        jnp.concatenate([w_qkv, w_out, narrow], axis=1), AXIS, axis=0, tiled=True
    )
    qkv_w, out_w = dense[:, : 3 * D], dense[:, 3 * D : 4 * D]
    router_w = dense[:, 4 * D : 4 * D + EXPERTS]
    gain_first = dense[:, 4 * D + EXPERTS].astype(F32)
    gain_second = dense[:, 4 * D + EXPERTS + 1].astype(F32)

    def weights_for(flip):
        return jnp.stack(
            [
                lax.dynamic_index_in_dim(expert_up, quad ^ flip, 1, False),
                lax.dynamic_index_in_dim(expert_down, quad ^ flip, 1, False),
            ]
        )

    mine = jnp.stack(swap_rows([weights_for(flip) for flip in range(EXPERTS)], size), axis=1)
    weights = lax.all_gather(
        mine.reshape(1, 2, EXPERTS * units, D),
        AXIS,
        axis=0,
        tiled=True,
        axis_index_groups=same_expert,
    )

    ends = jnp.cumsum(lengths[0])
    places = lax.iota(jnp.int32, TOK_DEV)
    doc_ids = jnp.sum((places[:, None] >= ends[None, :]).astype(jnp.int32), axis=1)
    spread = lax.iota(jnp.int32, TILE)
    offsets = (
        TILE * jnp.arange(-1, 2)[:, None, None] + spread[None, :, None] - spread[None, None, :]
    )
    buckets = bucket_of(offsets)
    near = jnp.zeros((HEADS, 3, TILE, TILE), F32)
    for bucket in range(BUCKETS):
        near = jnp.where(
            (buckets == bucket)[None], table[bucket].astype(F32)[:, None, None, None], near
        )
    extra_q, extra_k = score_extras(table, doc_ids)

    route = routes[:, 0]
    chosen = (route[:, None] == lax.iota(jnp.int32, EXPERTS)[None, :]).astype(jnp.int32)
    rank = jnp.sum((jnp.cumsum(chosen, axis=0) - chosen) * chosen, axis=1)
    slot = (route ^ quad) * CAP + rank
    route_hot = chosen.astype(F32)

    def dispatch(values):
        return jnp.zeros((ROWS, D), BF16).at[slot].set(values).reshape(EXPERTS, CAP, D)

    tokens_f = tokens.astype(F32)
    normed = rms_norm(tokens_f, gain_first).astype(BF16)
    qkv = jnp.dot(normed, qkv_w, preferred_element_type=F32).astype(BF16)
    late_cotangent, qkv = lax.optimization_barrier((cotangent, qkv))
    upstream_rows = jnp.concatenate(swap_rows(dispatch(late_cotangent), size))
    mixed, logs = attend(qkv, extra_q, extra_k, near)
    attended = tokens_f + jnp.dot(mixed, out_w, preferred_element_type=F32)
    normed_ffn = rms_norm(attended, gain_second).astype(BF16)
    rows = jnp.concatenate(swap_rows(dispatch(normed_ffn), size))
    logits = jnp.dot(normed_ffn, router_w, preferred_element_type=F32)
    probs_route = jax.nn.softmax(logits, axis=-1)
    gate = jnp.sum(probs_route * route_hot, axis=1, keepdims=True)
    gate_slots = jnp.sum(
        jnp.where(slot[None, :] == lax.iota(jnp.int32, ROWS)[:, None], gate[:, 0][None, :], 0.0),
        axis=1,
    ).reshape(EXPERTS, CAP)
    gate_rows = jnp.concatenate(swap_rows(gate_slots, size))
    grad_rows = (gate_rows[:, None] * upstream_rows.astype(F32)).astype(BF16)

    expert_rows, hidden, slopes = expert_forward(rows, weights)
    expert_tok = jnp.concatenate(swap_rows(expert_rows.reshape(EXPERTS, CAP, D), size))[
        slot
    ].astype(F32)
    back_rows, grad_pre = expert_backward(grad_rows, slopes, weights)
    back_tok = jnp.concatenate(swap_rows(back_rows.reshape(EXPERTS, CAP, D), size))[slot].astype(
        F32
    )
    expert_grads = expert_weight_grads(rows, grad_rows, hidden, grad_pre, weights)
    expert_sums = lax.psum_scatter(
        expert_grads, AXIS, scatter_dimension=0, tiled=True, axis_index_groups=same_expert
    ).reshape(2, EXPERTS, units, D)

    output = (attended + gate * expert_tok).astype(BF16)
    upstream = cotangent.astype(F32)
    grad_gate = jnp.sum(upstream * expert_tok, axis=1, keepdims=True)
    grad_logits = (probs_route * (grad_gate * route_hot - grad_gate * gate)).astype(BF16)
    grad_normed_ffn = back_tok + jnp.einsum(
        "te,de->td", grad_logits, router_w, preferred_element_type=F32
    )
    unused_second, second_pull = jax.vjp(rms_norm, attended, gain_second)
    grad_res_norm, grad_gain_second = second_pull(grad_normed_ffn)
    grad_res = upstream + grad_res_norm
    grad_attn_out = grad_res.astype(BF16)
    grad_mixed = jnp.einsum(
        "tf,df->td", grad_attn_out, out_w, preferred_element_type=F32
    ).astype(BF16)
    grad_w_out = jnp.einsum("td,tf->df", mixed, grad_attn_out, preferred_element_type=F32)
    grad_router = jnp.einsum("td,te->de", normed_ffn, grad_logits, preferred_element_type=F32)
    first_sums = scatter_sums(
        jnp.concatenate(
            [
                grad_w_out,
                grad_router,
                grad_gain_second[:, None],
                jnp.zeros((D, 128 - EXPERTS - 1), F32),
            ],
            axis=1,
        ),
        size,
    )

    grad_q, grad_k, grad_v, grad_table = attend_back(
        qkv, grad_mixed, logs, extra_q, extra_k, near, buckets
    )
    table_sum = sum_everywhere(
        jnp.sum(grad_table, axis=-1).reshape(HEADS, BUCKETS).T, size
    )
    grad_qkv = jnp.concatenate([grad_q, grad_k, grad_v], axis=1)
    grad_w_qkv = jnp.einsum("td,tf->df", normed, grad_qkv, preferred_element_type=F32)
    grad_normed = jnp.einsum("tf,df->td", grad_qkv, qkv_w, preferred_element_type=F32)
    unused_first, first_pull = jax.vjp(rms_norm, tokens_f, gain_first)
    grad_tok_norm, grad_gain_first = first_pull(grad_normed)
    grad_tokens = (grad_res + grad_tok_norm).astype(BF16)
    last_sums = scatter_sums(
        jnp.concatenate([grad_w_qkv, grad_gain_first[:, None], jnp.zeros((D, 127), F32)], axis=1),
        size,
    )

    by_flip = jnp.stack(
        swap_rows([expert_sums[:, flip] for flip in range(EXPERTS)], size), axis=2
    ).astype(F32)
    by_expert = jnp.concatenate(
        [lax.dynamic_slice_in_dim(by_flip, quad ^ expert, 1, 2) for expert in range(EXPERTS)],
        axis=2,
    )
    return (
        output,
        grad_tokens,
        last_sums[:, 3 * D],
        last_sums[:, : 3 * D],
        first_sums[:, :D],
        table_sum,
        first_sums[:, D + EXPERTS],
        first_sums[:, D : D + EXPERTS],
        by_expert[0],
        by_expert[1],
    )


def solution(mesh):
    rows = P(AXIS, None)
    in_specs = (
        rows, rows, rows, rows, P(AXIS), rows, rows, P(), P(AXIS), rows,
        P(AXIS, None, None), P(AXIS, None, None),
    )
    out_specs = (
        rows, rows, P(AXIS), rows, rows, P(), P(AXIS), rows,
        P(AXIS, None, None), P(AXIS, None, None),
    )
    return jax.shard_map(
        functools.partial(body, mesh.shape[AXIS]),
        mesh=mesh,
        in_specs=in_specs,
        out_specs=out_specs,
        check_vma=False,
    )
```

```python
import functools

import jax
import jax.numpy as jnp
from jax import lax
from jax.experimental import pallas as pl
from jax.experimental.pallas import tpu as pltpu
from jax.sharding import PartitionSpec as P

D = 768
HEADS = 12
HEAD_DIM = 64
PAIRS = HEADS // 2
PARTS = 3
PART_PAIRS = PAIRS // PARTS
PART = D // PARTS
BUCKETS = 32
EXPERTS = 4
TOK_DEV = 1024
CAP = 512
ROW_CHUNK = 256
ROWS = EXPERTS * CAP
AXIS = "fsdp"
F32 = jnp.float32
BF16 = jnp.bfloat16

norm_eps = 1e-06
masked_fill = -1e30
far_steps = (12, 16, 23, 32, 46, 64, 91)

TILE = 128
KEY_TILES = TOK_DEV // TILE
QUERY_BLOCK = 256
QUERY_BLOCKS = TOK_DEV // QUERY_BLOCK
HALVES = QUERY_BLOCK // TILE
NT = (((1,), (1,)), ((), ()))
NN = (((1,), (0,)), ((), ()))
TN = (((0,), (0,)), ((), ()))


def bucket_of(offset):
    distance = jnp.abs(offset)
    far_bucket = 8 + sum(((distance >= step).astype(jnp.int32) for step in far_steps))
    return jnp.where(distance < 8, distance, far_bucket) + 16 * (offset > 0).astype(jnp.int32)


def rms_norm(values, gain):
    return values * lax.rsqrt(jnp.mean(values * values, axis=-1, keepdims=True) + norm_eps) * gain


def along_z(value, size, shift):
    depth = size // 8
    return lax.ppermute(
        value, AXIS, [(i, (i // 8 + shift) % depth * 8 + i % 8) for i in range(size)]
    )


def along_quad(value, size, flip):
    return lax.ppermute(value, AXIS, [(i, i ^ (flip << 1)) for i in range(size)])


def along_core(value, size):
    return lax.ppermute(value, AXIS, [(i, i ^ 1) for i in range(size)])


def destinations(size, owned):
    me = lax.axis_index(AXIS)
    depth = size // 8
    z, quad, core = me // 8, me // 2 % 4, me % 2
    place = lax.iota(jnp.int32, size * owned)
    block, inner = place // owned, place % owned
    shift, flip, cross = block % depth, block // depth % 4, block // (depth * 4)
    owner = ((z + shift) % depth * 4 + (quad ^ flip)) * 2 + (core ^ cross)
    source = owner * owned + inner
    return (place[:, None] == source[None, :]).astype(BF16)


def for_quad(total):
    view = total.reshape(4, -1, total.shape[1])
    return [view[flip].astype(BF16) for flip in range(1, 4)], view


def add_z(total, size):
    depth = size // 8
    view = total.reshape(depth, -1, total.shape[1])
    out = view[0]
    for shift in range(1, depth):
        out = out + along_z(view[shift].astype(BF16), size, shift).astype(F32)
    return out


def sum_all(values):
    while len(values) > 1:
        values = [left + right for left, right in zip(values[::2], values[1::2])]
    return values[0]


def along_z_flip(value, size, flip):
    return lax.ppermute(value, AXIS, [(i, i ^ (flip << 3)) for i in range(size)])


def score_tile(tile, block, keys, queries, near_ref, head):
    scores = lax.dot_general(
        keys[tile * TILE : (tile + 1) * TILE], queries, NT, preferred_element_type=F32
    )
    parts = []
    for half in range(HALVES):
        part = scores[:, half * TILE : (half + 1) * TILE]
        apart = tile - (block * HALVES + half)
        if abs(apart) <= 1:
            part = part + near_ref[head, apart + 1]
        parts.append(part)
    return parts


def fold(value, combine):
    return combine(value.reshape(value.shape[0] // 8, 8, value.shape[1]), axis=0)


def attend_kernel(
    q_ref, k_ref, v_ref, extra_q_ref, extra_k_ref, near_ref, out_ref, log_ref,
    score_ref, prob_ref, turned_ref,
):
    lane = lax.broadcasted_iota(jnp.int32, (TOK_DEV, 2 * HEAD_DIM), 1)
    queries = (q_ref[...].astype(F32) * 0.125).astype(BF16)
    keys = k_ref[...]
    values_t = v_ref[...].astype(F32).T.astype(BF16)
    for head in range(2):
        own = (lane < HEAD_DIM) if head == 0 else (lane >= HEAD_DIM)
        head_keys = jnp.where(own, keys, extra_k_ref[head])
        head_queries = jnp.where(own, queries, extra_q_ref[head])
        head_values = values_t[head * HEAD_DIM : (head + 1) * HEAD_DIM]
        for block in range(QUERY_BLOCKS):
            side = block % 2
            at = slice(block * QUERY_BLOCK, (block + 1) * QUERY_BLOCK)
            top = None
            for tile in range(KEY_TILES):
                parts = score_tile(tile, block, head_keys, head_queries[at], near_ref, head)
                highs = []
                for half, part in enumerate(parts):
                    score_ref[
                        side, tile * TILE : (tile + 1) * TILE, half * TILE : (half + 1) * TILE
                    ] = part
                    highs.append(fold(part, jnp.max))
                high = jnp.concatenate(highs, axis=1)
                top = high if top is None else jnp.maximum(top, high)
            top = jnp.max(top, axis=0, keepdims=True)
            total = jnp.zeros((8, QUERY_BLOCK), F32)
            for tile in range(KEY_TILES):
                rows = slice(tile * TILE, (tile + 1) * TILE)
                expo = jnp.exp(score_ref[side, rows, :] - top)
                total = total + fold(expo, jnp.sum)
                prob_ref[side, rows, :] = expo.astype(BF16)
            total = jnp.sum(total, axis=0, keepdims=True)
            mixed = lax.dot_general(head_values, prob_ref[side], NN, preferred_element_type=F32)
            turned_ref[head * HEAD_DIM : (head + 1) * HEAD_DIM, at] = mixed * (1.0 / total)
            log_ref[0, head : head + 1, at] = top + jnp.log(total)
    out_ref[...] = turned_ref[...].T.astype(BF16)


def attend_back_kernel(
    q_ref, k_ref, v_ref, grad_ref, log_ref, extra_q_ref, extra_k_ref, near_ref, bucket_ref,
    grad_qkv_ref, grad_table_ref,
    prob_ref, slope_ref, low_prob_ref, low_grad_ref, turned_ref, key_sum_ref, value_sum_ref,
    near_sum_ref,
):
    lane = lax.broadcasted_iota(jnp.int32, (TOK_DEV, 2 * HEAD_DIM), 1)
    queries = (q_ref[...].astype(F32) * 0.125).astype(BF16)
    keys = k_ref[...]
    keys_t = (keys.astype(F32) * 0.125).T.astype(BF16)
    values = v_ref[...]
    grads = grad_ref[...]
    zero = jnp.zeros_like(grads)
    for head in range(2):
        own = (lane < HEAD_DIM) if head == 0 else (lane >= HEAD_DIM)
        head_keys = jnp.where(own, keys, extra_k_ref[head])
        head_queries = jnp.where(own, queries, extra_q_ref[head])
        bare_queries = jnp.where(own, queries, zero)
        head_grads = jnp.where(own, grads, zero)
        head_keys_t = keys_t[head * HEAD_DIM : (head + 1) * HEAD_DIM]
        near_sum_ref[...] = jnp.zeros_like(near_sum_ref)
        far_sums = [jnp.zeros((8, TILE), F32), jnp.zeros((8, TILE), F32)]
        for block in range(QUERY_BLOCKS):
            side = block % 2
            at = slice(block * QUERY_BLOCK, (block + 1) * QUERY_BLOCK)
            logs = log_ref[0, head : head + 1, at]
            delta = jnp.zeros((8, QUERY_BLOCK), F32)
            for tile in range(KEY_TILES):
                rows = slice(tile * TILE, (tile + 1) * TILE)
                parts = score_tile(tile, block, head_keys, head_queries[at], near_ref, head)
                probs = jnp.exp(jnp.concatenate(parts, axis=1) - logs)
                slopes = lax.dot_general(
                    values[rows], head_grads[at], NT, preferred_element_type=F32
                )
                delta = delta + fold(probs * slopes, jnp.sum)
                prob_ref[side, rows, :] = probs
                low_prob_ref[side, rows, :] = probs.astype(BF16)
                slope_ref[side, rows, :] = slopes
            delta = jnp.sum(delta, axis=0, keepdims=True)
            for tile in range(KEY_TILES):
                rows = slice(tile * TILE, (tile + 1) * TILE)
                grad_scores = prob_ref[side, rows, :] * (slope_ref[side, rows, :] - delta)
                low_grad_ref[side, rows, :] = grad_scores.astype(BF16)
                for half in range(HALVES):
                    part = grad_scores[:, half * TILE : (half + 1) * TILE]
                    apart = tile - (block * HALVES + half)
                    if abs(apart) <= 1:
                        near_sum_ref[apart + 1] += part
                    else:
                        which = 0 if apart < 0 else 1
                        far_sums[which] = far_sums[which] + fold(part, jnp.sum)
            value_part = lax.dot_general(
                low_prob_ref[side], head_grads[at], NN, preferred_element_type=F32
            )
            key_part = lax.dot_general(
                low_grad_ref[side], bare_queries[at], NN, preferred_element_type=F32
            )
            if head == 0 and block == 0:
                value_sum_ref[...] = value_part
                key_sum_ref[...] = key_part
            else:
                value_sum_ref[...] += value_part
                key_sum_ref[...] += key_part
            turned_ref[head * HEAD_DIM : (head + 1) * HEAD_DIM, at] = lax.dot_general(
                head_keys_t, low_grad_ref[side], NN, preferred_element_type=F32
            )
        for bucket in range(BUCKETS):
            row = jnp.zeros((8, TILE), F32)
            for apart in (-1, 0, 1):
                if (apart < 0 and bucket >= 16) or (apart > 0 and bucket < 16):
                    continue
                picked = jnp.where(
                    bucket_ref[apart + 1] == bucket, near_sum_ref[apart + 1], 0.0
                )
                row = row + fold(picked, jnp.sum)
            if bucket == 15:
                row = row + far_sums[0]
            if bucket == 31:
                row = row + far_sums[1]
            grad_table_ref[0, head, bucket : bucket + 1, :] = jnp.sum(row, axis=0, keepdims=True)
    grad_qkv_ref[0] = turned_ref[...].T.astype(BF16)
    grad_qkv_ref[1] = key_sum_ref[...].astype(BF16)
    grad_qkv_ref[2] = value_sum_ref[...].astype(BF16)


def column(first):
    return pl.BlockSpec((TOK_DEV, 2 * HEAD_DIM), lambda pair: (0, first + pair))


def score_specs(first):
    return [
        pl.BlockSpec((2, TOK_DEV, 2 * HEAD_DIM), lambda pair: (0, 0, 0)),
        pl.BlockSpec((2, TOK_DEV, 2 * HEAD_DIM), lambda pair: (first + pair, 0, 0)),
        pl.BlockSpec((2, 3, TILE, TILE), lambda pair: (first + pair, 0, 0, 0)),
    ]


def attend(qkv, extra_q, extra_k, near):
    logs = pl.BlockSpec((1, 2, TOK_DEV), lambda pair: (pair, 0, 0))
    return pl.pallas_call(
        attend_kernel,
        grid=(PAIRS,),
        in_specs=[column(0), column(PAIRS), column(2 * PAIRS)] + score_specs(0),
        out_specs=[column(0), logs],
        out_shape=[
            jax.ShapeDtypeStruct((TOK_DEV, D), BF16),
            jax.ShapeDtypeStruct((PAIRS, 2, TOK_DEV), F32),
        ],
        scratch_shapes=[
            pltpu.VMEM((2, TOK_DEV, QUERY_BLOCK), F32),
            pltpu.VMEM((2, TOK_DEV, QUERY_BLOCK), BF16),
            pltpu.VMEM((2 * HEAD_DIM, TOK_DEV), F32),
        ],
        compiler_params=pltpu.CompilerParams(vmem_limit_bytes=40 << 20),
        cost_estimate=pl.CostEstimate(
            flops=40_000_000_000, bytes_accessed=12 << 20, transcendentals=HEADS << 20
        ),
    )(qkv, qkv, qkv, extra_q, extra_k, near)


def attend_back(part, qkv, grad_mixed, logs, extra_q, extra_k, near, buckets):
    first = part * PART_PAIRS
    return pl.pallas_call(
        attend_back_kernel,
        grid=(PART_PAIRS,),
        in_specs=[
            column(first),
            column(PAIRS + first),
            column(2 * PAIRS + first),
            column(first),
            pl.BlockSpec((1, 2, TOK_DEV), lambda pair: (first + pair, 0, 0)),
        ]
        + score_specs(first)
        + [pl.BlockSpec((3, TILE, TILE), lambda pair: (0, 0, 0))],
        out_specs=[
            pl.BlockSpec((3, TOK_DEV, 2 * HEAD_DIM), lambda pair: (0, 0, pair)),
            pl.BlockSpec((1, 2, BUCKETS, TILE), lambda pair: (pair, 0, 0, 0)),
        ],
        out_shape=[
            jax.ShapeDtypeStruct((3, TOK_DEV, PART), BF16),
            jax.ShapeDtypeStruct((PART_PAIRS, 2, BUCKETS, TILE), F32),
        ],
        scratch_shapes=[
            pltpu.VMEM((2, TOK_DEV, QUERY_BLOCK), F32),
            pltpu.VMEM((2, TOK_DEV, QUERY_BLOCK), F32),
            pltpu.VMEM((2, TOK_DEV, QUERY_BLOCK), BF16),
            pltpu.VMEM((2, TOK_DEV, QUERY_BLOCK), BF16),
            pltpu.VMEM((2 * HEAD_DIM, TOK_DEV), F32),
            pltpu.VMEM((TOK_DEV, 2 * HEAD_DIM), F32),
            pltpu.VMEM((TOK_DEV, 2 * HEAD_DIM), F32),
            pltpu.VMEM((3, TILE, TILE), F32),
        ],
        compiler_params=pltpu.CompilerParams(vmem_limit_bytes=48 << 20),
        cost_estimate=pl.CostEstimate(
            flops=80_000_000_000 // PARTS,
            bytes_accessed=8 << 20,
            transcendentals=(HEADS << 20) // PARTS,
        ),
    )(qkv, qkv, qkv, grad_mixed, logs, extra_q, extra_k, near, buckets)


def score_extras(table, doc_ids):
    lane = lax.iota(jnp.int32, HEAD_DIM)
    places = lax.iota(jnp.int32, TOK_DEV)
    tiles = places // TILE
    is_doc = lane < 4
    block_lane = (lane >= 4) & (lane < 4 + KEY_TILES)
    same = doc_ids[:, None] == lane[None, :]
    in_block = tiles[:, None] == (lane - 4)[None, :]
    extra_q = jnp.where((is_doc & same) | (block_lane & in_block), 1.0, 0.0).astype(BF16)
    apart = tiles[:, None] - (lane - 4)[None, :]
    mask_k = jnp.where(is_doc & ~same, masked_fill, 0.0)
    far = jnp.where(
        apart[None] < 0, table[15].astype(F32)[:, None, None], table[31].astype(F32)[:, None, None]
    )
    use_far = (block_lane & (jnp.abs(apart) > 1))[None]
    extra_k = jnp.where(use_far, far, mask_k[None]).astype(BF16)
    blank = jnp.zeros_like(extra_q)
    queries = jnp.stack(
        [jnp.concatenate([blank, extra_q], axis=1), jnp.concatenate([extra_q, blank], axis=1)]
    )
    pairs = extra_k.reshape(PAIRS, 2, TOK_DEV, HEAD_DIM)
    even = jnp.concatenate([jnp.zeros_like(pairs[:, 0]), pairs[:, 0]], axis=-1)
    odd = jnp.concatenate([pairs[:, 1], jnp.zeros_like(pairs[:, 1])], axis=-1)
    keys = jnp.stack([even, odd], axis=1).reshape(HEADS, TOK_DEV, 2 * HEAD_DIM)
    return queries, keys


def gelu_with_slope(x):
    scale, cubic = 0.7978845608028654, 0.044715
    square = x * x
    half = 0.5 + 0.5 * jnp.tanh(x * (scale + (scale * cubic) * square))
    value = x * half
    slope = half + value * (1.0 - half) * (2.0 * scale + (6.0 * scale * cubic) * square)
    return value, slope


def expert_kernel(
    rows_ref, upstream_ref, gate_ref, up_ref, down_ref,
    out_ref, back_ref, grad_ref, hidden_ref, grad_pre_ref, out_sum_ref, back_sum_ref,
):
    step = pl.program_id(0)
    up = up_ref[...].reshape(-1, D)
    down = down_ref[...].reshape(-1, D)

    @pl.when(step == 0)
    def _():
        out_sum_ref[...] = jnp.zeros_like(out_sum_ref)
        back_sum_ref[...] = jnp.zeros_like(back_sum_ref)
        gate = jnp.broadcast_to(gate_ref[...], (TILE, CAP)).T
        for first in range(0, D, TILE):
            lanes = slice(first, first + TILE)
            grad_ref[:, lanes] = (gate * upstream_ref[:, lanes].astype(F32)).astype(BF16)

    for first in range(0, CAP, ROW_CHUNK):
        at = slice(first, first + ROW_CHUNK)
        pre = lax.dot_general(rows_ref[at], up, NT, preferred_element_type=F32)
        grad_hidden = lax.dot_general(grad_ref[at], down, NT, preferred_element_type=F32)
        hidden, slope = gelu_with_slope(pre)
        hidden = hidden.astype(BF16)
        grad_pre = (grad_hidden * slope).astype(BF16)
        hidden_ref[at] = hidden
        grad_pre_ref[at] = grad_pre
        out_sum_ref[at] += lax.dot_general(hidden, down, NN, preferred_element_type=F32)
        back_sum_ref[at] += lax.dot_general(grad_pre, up, NN, preferred_element_type=F32)

    @pl.when(step == pl.num_programs(0) - 1)
    def _():
        out_ref[...] = out_sum_ref[...].astype(BF16)
        back_ref[...] = back_sum_ref[...].astype(BF16)


def expert_weight_kernel(*refs):
    out_ref = refs[-1]
    rows, grads, hiddens, grad_pres = (refs[EXPERTS * i : EXPERTS * (i + 1)] for i in range(4))
    pieces, _, units, _ = out_ref.shape
    for which, lefts, rights in ((0, grad_pres, rows), (1, hiddens, grads)):
        total = None
        for left_ref, right_ref in zip(lefts, rights):
            part = lax.dot_general(
                left_ref[...], right_ref[...], TN, preferred_element_type=F32
            )
            total = part if total is None else total + part
        out_ref[:, which] = total.astype(BF16).reshape(pieces, units, D)


def weight_kernel(left_ref, right_ref, mine_ref, other_ref):
    half = D // 2
    for which in range(right_ref.shape[0]):
        width = right_ref.shape[2]
        lanes = slice(which * width, (which + 1) * width)
        for first, out_ref in ((0, mine_ref), (half, other_ref)):
            part = lax.dot_general(
                left_ref[:, first : first + half],
                right_ref[which],
                TN,
                preferred_element_type=F32,
            )
            out_ref[:, lanes] = part.astype(out_ref.dtype)


def weight_halves(left, right):
    width = right.shape[0] * right.shape[2]
    whole = pl.BlockSpec((TOK_DEV, D), lambda step: (0, 0))
    out = pl.BlockSpec((D // 2, width), lambda step: (0, 0))
    return pl.pallas_call(
        weight_kernel,
        grid=(1,),
        in_specs=[whole, pl.BlockSpec(right.shape, lambda step: (0, 0, 0))],
        out_specs=[out, out],
        out_shape=[
            jax.ShapeDtypeStruct((D // 2, width), F32),
            jax.ShapeDtypeStruct((D // 2, width), BF16),
        ],
        compiler_params=pltpu.CompilerParams(vmem_limit_bytes=40 << 20),
        cost_estimate=pl.CostEstimate(
            flops=2 * TOK_DEV * D * width, bytes_accessed=6 << 20, transcendentals=0
        ),
    )(left, right)


def token_grad_kernel(
    grads_0, grads_1, grads_2, weights_0, weights_1, weights_2, tokens_ref, gain_ref, rest_ref,
    out_ref,
):
    grad = None
    for grads_ref, weights_ref in zip(
        (grads_0, grads_1, grads_2), (weights_0, weights_1, weights_2)
    ):
        for which in range(3):
            part = lax.dot_general(
                grads_ref[which],
                weights_ref[:, which * PART : (which + 1) * PART],
                NT,
                preferred_element_type=F32,
            )
            grad = part if grad is None else grad + part
    values = tokens_ref[...].astype(F32)
    grad = grad * gain_ref[...]
    inverse = lax.rsqrt(jnp.mean(values * values, axis=-1, keepdims=True) + norm_eps)
    along = jnp.mean(values * grad, axis=-1, keepdims=True)
    out_ref[...] = (
        rest_ref[...] + inverse * (grad - values * (inverse * inverse * along))
    ).astype(BF16)


def token_grad(grads, weights, tokens, gain, rest):
    rows = TOK_DEV // 4
    part = pl.BlockSpec((rows, D), lambda step: (step, 0))
    return pl.pallas_call(
        token_grad_kernel,
        grid=(TOK_DEV // rows,),
        in_specs=[pl.BlockSpec((3, rows, PART), lambda step: (0, step, 0))] * PARTS
        + [pl.BlockSpec((D, 3 * PART), lambda step: (0, 0))] * PARTS
        + [part, pl.BlockSpec((1, D), lambda step: (0, 0)), part],
        out_specs=part,
        out_shape=jax.ShapeDtypeStruct((TOK_DEV, D), BF16),
        compiler_params=pltpu.CompilerParams(vmem_limit_bytes=48 << 20),
        cost_estimate=pl.CostEstimate(
            flops=6 * TOK_DEV * D * D, bytes_accessed=14 << 20, transcendentals=0
        ),
    )(*grads, *weights, tokens, gain, rest)


def early_kernel(
    slot_ref, values_ref, bucket_ref, table_ref, out_0, out_1, out_2, out_3, near_ref
):
    dispatch_kernel(slot_ref, values_ref, None, out_0, out_1, out_2, out_3)

    def fill(head, carry):
        for apart, first, last in ((0, 1, 16), (1, 0, BUCKETS), (2, 17, BUCKETS)):
            buckets = bucket_ref[apart]
            tile = jnp.zeros((TILE, TILE), F32)
            for bucket in range(first, last):
                tile = jnp.where(buckets == bucket, table_ref[bucket, head], tile)
            near_ref[head, apart] = tile
        return carry

    lax.fori_loop(0, HEADS, fill, 0)


def early(slot_row, values, buckets, table):
    vmem = pl.BlockSpec(memory_space=pltpu.VMEM)
    result = pl.pallas_call(
        early_kernel,
        in_specs=[vmem, vmem, vmem, pl.BlockSpec(memory_space=pltpu.SMEM)],
        out_shape=[jax.ShapeDtypeStruct((CAP, D), BF16)] * EXPERTS
        + [jax.ShapeDtypeStruct((HEADS, 3, TILE, TILE), F32)],
        compiler_params=pltpu.CompilerParams(vmem_limit_bytes=40 << 20),
        cost_estimate=pl.CostEstimate(
            flops=8 * ROWS * TOK_DEV * D, bytes_accessed=6 << 20, transcendentals=0
        ),
    )(slot_row, values, buckets, table)
    return list(result[:EXPERTS]), result[EXPERTS]


def dispatch_kernel(slot_ref, values_ref, gate_ref, out_0, out_1, out_2, out_3, *gate_outs):
    values = values_ref[...]
    for chunk, out_ref in enumerate((out_0, out_1, out_2, out_3)):
        wanted = chunk * CAP + lax.broadcasted_iota(jnp.int32, (CAP, TOK_DEV), 0)
        hit = wanted == slot_ref[...]
        out_ref[...] = lax.dot_general(
            jnp.where(hit, 1.0, 0.0).astype(BF16), values, NN, preferred_element_type=F32
        ).astype(BF16)
        if gate_outs:
            gates = jnp.sum(jnp.where(hit, gate_ref[...], 0.0), axis=1, keepdims=True)
            gate_outs[chunk][...] = jnp.broadcast_to(gates, (CAP, TILE)).T[0:1]


def dispatch(slot_row, values, gate_row):
    result = pl.pallas_call(
        dispatch_kernel,
        out_shape=[jax.ShapeDtypeStruct((CAP, D), BF16)] * EXPERTS
        + [jax.ShapeDtypeStruct((1, CAP), F32)] * EXPERTS,
        compiler_params=pltpu.CompilerParams(vmem_limit_bytes=40 << 20),
        cost_estimate=pl.CostEstimate(
            flops=2 * ROWS * TOK_DEV * D, bytes_accessed=6 << 20, transcendentals=0
        ),
    )(slot_row, values, gate_row)
    return list(result[:EXPERTS]), list(result[EXPERTS:])


def combine_kernel(slot_ref, *refs):
    rows = slot_ref.shape[0]
    totals = [None, None]
    for chunk in range(EXPERTS):
        place = chunk * CAP + lax.broadcasted_iota(jnp.int32, (rows, CAP), 1)
        hit = jnp.where(place == slot_ref[...], 1.0, 0.0).astype(BF16)
        for which in range(2):
            part = lax.dot_general(
                hit, refs[which * EXPERTS + chunk][...], NN, preferred_element_type=F32
            )
            totals[which] = part if totals[which] is None else totals[which] + part
    for which in range(2):
        refs[2 * EXPERTS + which][...] = totals[which]


def combine(slot_column, first, second):
    rows = TOK_DEV // 4
    part = pl.BlockSpec((rows, D), lambda step: (step, 0))
    return pl.pallas_call(
        combine_kernel,
        grid=(TOK_DEV // rows,),
        in_specs=[pl.BlockSpec((rows, 1), lambda step: (step, 0))]
        + [pl.BlockSpec((CAP, D), lambda step: (0, 0))] * (2 * EXPERTS),
        out_specs=[part, part],
        out_shape=[jax.ShapeDtypeStruct((TOK_DEV, D), F32)] * 2,
        compiler_params=pltpu.CompilerParams(vmem_limit_bytes=60 << 20),
        cost_estimate=pl.CostEstimate(
            flops=4 * ROWS * TOK_DEV * D, bytes_accessed=12 << 20, transcendentals=0
        ),
    )(slot_column, *first, *second)


def expert_layout(weights):
    pieces, _, units, _ = weights.shape
    per_step = max(1, D // units)
    steps = pieces // per_step
    width = per_step * units
    whole = pl.BlockSpec((CAP, D), lambda step: (0, 0))
    part = pl.BlockSpec((CAP, width), lambda step: (0, step))
    up = pl.BlockSpec((per_step, 1, units, D), lambda step: (step, 0, 0, 0))
    down = pl.BlockSpec((per_step, 1, units, D), lambda step: (step, 1, 0, 0))
    both = pl.BlockSpec((per_step, 2, units, D), lambda step: (step, 0, 0, 0))
    return steps, steps * width, whole, part, up, down, both


def expert_pass(rows, upstream, gate, weights):
    steps, total, whole, part, up, down, _ = expert_layout(weights)
    return pl.pallas_call(
        expert_kernel,
        grid=(steps,),
        in_specs=[whole, whole, pl.BlockSpec((1, CAP), lambda step: (0, 0)), up, down],
        out_specs=[whole, whole, whole, part, part],
        out_shape=[jax.ShapeDtypeStruct((CAP, D), BF16)] * 3
        + [jax.ShapeDtypeStruct((CAP, total), BF16)] * 2,
        scratch_shapes=[pltpu.VMEM((CAP, D), F32)] * 2,
        compiler_params=pltpu.CompilerParams(vmem_limit_bytes=48 << 20),
        cost_estimate=pl.CostEstimate(
            flops=8 * CAP * D * total, bytes_accessed=20 << 20, transcendentals=CAP * total
        ),
    )(rows, upstream, gate, weights, weights)


def expert_weight_grads(rows, grads, hiddens, grad_pres, weights):
    steps, total, whole, part, _, _, both = expert_layout(weights)
    return pl.pallas_call(
        expert_weight_kernel,
        grid=(steps,),
        in_specs=[whole] * (2 * EXPERTS) + [part] * (2 * EXPERTS),
        out_specs=both,
        out_shape=jax.ShapeDtypeStruct(weights.shape, BF16),
        compiler_params=pltpu.CompilerParams(vmem_limit_bytes=56 << 20),
        cost_estimate=pl.CostEstimate(
            flops=4 * ROWS * D * total, bytes_accessed=40 << 20, transcendentals=0
        ),
    )(*rows, *grads, *hiddens, *grad_pres)


def swap_rows(pieces, size):
    return [pieces[0]] + [along_quad(pieces[flip], size, flip) for flip in range(1, EXPERTS)]


def body(
    size,
    tokens,
    cotangent,
    lengths,
    routes,
    gain_attn,
    w_qkv,
    w_out,
    table,
    gain_ffn,
    router,
    expert_up,
    expert_down,
):
    quad = lax.axis_index(AXIS) // 2 % 4
    owned = w_qkv.shape[0]
    units = expert_up.shape[0]
    depth = size // 8
    same_expert = [
        [8 * z + 2 * q + c for z in range(depth) for c in range(2)] for q in range(EXPERTS)
    ]

    narrow = jnp.concatenate(
        [router, gain_attn[:, None], gain_ffn[:, None], jnp.zeros((owned, 128 - EXPERTS - 2), BF16)],
        axis=1,
    )
    owned_dense = jnp.concatenate([w_qkv, w_out, narrow], axis=1)
    z_dense = [along_z(owned_dense, size, -shift) for shift in range(1, depth)]
    hand_on = destinations(size, owned)
    turned_tokens = jnp.dot(tokens, hand_on, preferred_element_type=F32)

    def weights_for(flip):
        return jnp.stack(
            [
                lax.dynamic_index_in_dim(expert_up, quad ^ flip, 1, False),
                lax.dynamic_index_in_dim(expert_down, quad ^ flip, 1, False),
            ]
        )

    arrived_weights = swap_rows([weights_for(flip) for flip in range(EXPERTS)], size)
    ends = jnp.cumsum(lengths[0])
    places = lax.iota(jnp.int32, TOK_DEV)
    doc_ids = jnp.sum((places[:, None] >= ends[None, :]).astype(jnp.int32), axis=1)
    spread = lax.iota(jnp.int32, TILE)
    offsets = (
        TILE * jnp.arange(-1, 2)[:, None, None] + spread[None, :, None] - spread[None, None, :]
    )
    buckets = bucket_of(offsets)
    extra_q, extra_k = score_extras(table, doc_ids)

    route = routes[:, 0]
    chosen = (route[:, None] == lax.iota(jnp.int32, EXPERTS)[None, :]).astype(jnp.int32)
    rank = jnp.sum((jnp.cumsum(chosen, axis=0) - chosen) * chosen, axis=1)
    slot = (route ^ quad) * CAP + rank
    slot_row, slot_column = slot[None, :], slot[:, None]
    route_hot = chosen.astype(F32)

    tokens_f = tokens.astype(F32)
    (
        z_dense, arrived_weights, slot_row, buckets, extra_q, extra_k, turned_tokens, hand_on
    ) = lax.optimization_barrier(
        (
            z_dense, arrived_weights, slot_row, buckets, extra_q, extra_k, turned_tokens,
            hand_on,
        )
    )
    mine = jnp.stack(arrived_weights, axis=1)
    weights = lax.all_gather(
        mine.reshape(1, 2, EXPERTS * units, D),
        AXIS,
        axis=0,
        tiled=True,
        axis_index_groups=same_expert,
    )
    quad_dense = jnp.concatenate([owned_dense] + z_dense)
    arrived_dense = [along_quad(quad_dense, size, flip) for flip in range(1, 4)]
    (upstream_rows, near), arrived_dense = lax.optimization_barrier(
        (early(slot_row, cotangent, buckets, table.astype(F32)), arrived_dense)
    )
    core_dense = jnp.concatenate([quad_dense] + arrived_dense)
    dense = jnp.concatenate([core_dense, along_core(core_dense, size)])
    turned_gain = dense[:, 4 * D + EXPERTS].astype(F32)
    turned_normed = rms_norm(turned_tokens, turned_gain).astype(BF16)
    qkv = jnp.dot(turned_normed, dense[:, : 3 * D], preferred_element_type=F32).astype(BF16)
    upstream_rows, qkv = lax.optimization_barrier((upstream_rows, qkv))
    upstream_rows = swap_rows(upstream_rows, size)
    side = jnp.dot(hand_on, dense[:, 3 * D :], preferred_element_type=F32).astype(BF16)
    side, qkv = lax.optimization_barrier((side, qkv))
    out_w = side[:, :D]
    router_w = side[:, D : D + EXPERTS]
    gain_first = side[:, D + EXPERTS].astype(F32)
    gain_second = side[:, D + EXPERTS + 1].astype(F32)
    mixed, logs = attend(qkv, extra_q, extra_k, near)
    mixed, upstream_rows = lax.optimization_barrier((mixed, upstream_rows))
    attended = tokens_f + jnp.dot(mixed, out_w, preferred_element_type=F32)
    normed_ffn = rms_norm(attended, gain_second).astype(BF16)
    logits = jnp.dot(normed_ffn, router_w, preferred_element_type=F32)
    probs_route = jax.nn.softmax(logits, axis=-1)
    gate = jnp.sum(probs_route * route_hot, axis=1, keepdims=True)
    rows, gates = dispatch(slot_row, normed_ffn, gate.reshape(1, TOK_DEV))
    rows[0], late_mixed, late_dense = lax.optimization_barrier((rows[0], mixed, dense))
    gates = swap_rows(gates, size)
    rows[1], rows[2] = along_quad(rows[1], size, 1), along_quad(rows[2], size, 2)
    turned_mixed = jnp.dot(late_mixed, hand_on, preferred_element_type=F32).astype(BF16)
    qkv_parts = [
        jnp.dot(
            hand_on,
            jnp.concatenate(
                [
                    late_dense[:, which * D + part * PART : which * D + (part + 1) * PART]
                    for which in range(3)
                ],
                axis=1,
            ),
            preferred_element_type=F32,
        ).astype(BF16)
        for part in range(PARTS)
    ]
    rows[1], rows[3], gates, turned_mixed, qkv_parts = lax.optimization_barrier(
        (rows[1], rows[3], gates, turned_mixed, qkv_parts)
    )
    rows[3] = along_quad(rows[3], size, 3)

    def run(flip, rows_in):
        return list(expert_pass(rows_in, upstream_rows[flip], gates[flip], weights))

    def out_of(flip, which):
        return along_quad(passes[flip][which], size, flip)

    passes = {}
    passes[1] = run(1, rows[1])
    rows_2, passes[1][2] = lax.optimization_barrier((rows[2], passes[1][2]))
    out_1 = out_of(1, 0)
    passes[2] = run(2, rows_2)
    passes[2][2], out_1 = lax.optimization_barrier((passes[2][2], out_1))
    rows_3, passes[2][2] = lax.optimization_barrier((rows[3], passes[2][2]))
    back_1, out_2 = out_of(1, 1), out_of(2, 0)
    passes[3] = run(3, rows_3)
    passes[3][2], back_1, out_2 = lax.optimization_barrier((passes[3][2], back_1, out_2))
    rows_0, passes[3][2] = lax.optimization_barrier((rows[0], passes[3][2]))
    back_2 = out_of(2, 1)
    passes[0] = run(0, rows_0)
    passes[0][2], back_2 = lax.optimization_barrier((passes[0][2], back_2))
    out_3, back_3 = out_of(3, 0), out_of(3, 1)
    order = [passes[flip] for flip in range(EXPERTS)]
    expert_grads = expert_weight_grads(
        rows, *([member[which] for member in order] for which in (2, 3, 4)), weights
    )
    expert_grads, out_3, back_3 = lax.optimization_barrier((expert_grads, out_3, back_3))
    expert_tok, back_tok = combine(
        slot_column,
        (passes[0][0], out_1, out_2, out_3),
        (passes[0][1], back_1, back_2, back_3),
    )
    expert_sums = lax.psum_scatter(
        expert_grads, AXIS, scatter_dimension=0, tiled=True, axis_index_groups=same_expert
    ).reshape(2, EXPERTS, units, D)

    output = (attended + gate * expert_tok).astype(BF16)
    upstream = cotangent.astype(F32)
    grad_gate = jnp.sum(upstream * expert_tok, axis=1, keepdims=True)
    grad_logits = (probs_route * (grad_gate * route_hot - grad_gate * gate)).astype(BF16)
    grad_normed_ffn = back_tok + jnp.einsum(
        "te,de->td", grad_logits, router_w, preferred_element_type=F32
    )
    unused_second, second_pull = jax.vjp(rms_norm, attended, gain_second)
    grad_res_norm, grad_gain_second = second_pull(grad_normed_ffn)
    grad_res = upstream + grad_res_norm
    grad_attn_out = grad_res.astype(BF16)
    grad_mixed = jnp.einsum(
        "tf,df->td", grad_attn_out, out_w, preferred_element_type=F32
    ).astype(BF16)
    grad_router = jnp.einsum("td,te->de", normed_ffn, grad_logits, preferred_element_type=F32)

    narrow = jnp.concatenate(
        [grad_router, grad_gain_second[:, None], jnp.zeros((D, 128 - EXPERTS - 1), F32)], axis=1
    ).astype(BF16)
    narrow = lax.dot_general(hand_on, narrow, TN, preferred_element_type=F32)
    narrow_mine, narrow_other = narrow[: D // 2], narrow[D // 2 :].astype(BF16)
    out_mine, out_other = weight_halves(turned_mixed, grad_attn_out[None])

    def attend_part(part, logs):
        return attend_back(part, qkv, grad_mixed, logs, extra_q, extra_k, near, buckets)

    grads_0, table_0 = attend_part(0, logs)
    mine, other = weight_halves(turned_normed, grads_0)
    other = jnp.concatenate([out_other, narrow_other, other], axis=1)
    mine = jnp.concatenate([out_mine, narrow_mine, mine], axis=1)
    logs, other, mine = lax.optimization_barrier((logs, other, mine))
    arrived = along_core(other, size)
    (grads_1, table_1), arrived = lax.optimization_barrier((attend_part(1, logs), arrived))
    low, view = for_quad(mine + arrived.astype(F32))
    mine_1, other_1 = weight_halves(turned_normed, grads_1)
    logs, low, view, other_1, mine_1 = lax.optimization_barrier(
        (logs, low, view, other_1, mine_1)
    )
    arrived_1 = along_core(other_1, size)
    arrived = [along_quad(low[flip - 1], size, flip) for flip in range(1, 4)]
    (grads_2, table_2), arrived, arrived_1, expert_sums = lax.optimization_barrier(
        (attend_part(2, logs), arrived, arrived_1, expert_sums)
    )
    mine_2, other_2 = weight_halves(turned_normed, grads_2)
    table_grad = jnp.concatenate(
        [
            jnp.sum(part, axis=-1).reshape(HEADS // PARTS, BUCKETS)
            for part in (table_0, table_1, table_2)
        ]
    ).reshape(-1, 128)
    other_2, mine_2, table_grad, expert_sums = lax.optimization_barrier(
        (other_2, mine_2, table_grad, expert_sums)
    )
    by_flip = swap_rows([expert_sums[:, flip] for flip in range(EXPERTS)], size)

    arrived_2 = along_core(other_2, size)
    table_grad = table_grad + along_core(table_grad, size)
    total = view[0] + sum(piece.astype(F32) for piece in arrived)
    late_1 = mine_1 + arrived_1.astype(F32)
    arrived_2, table_grad, total, late_1 = lax.optimization_barrier(
        (arrived_2, table_grad, total, late_1)
    )
    low, view = for_quad(
        jnp.concatenate([late_1, mine_2 + arrived_2.astype(F32)], axis=1)
    )
    low, view, late_grads = lax.optimization_barrier((low, view, [grads_0, grads_1, grads_2]))
    arrived = [along_quad(low[flip - 1], size, flip) for flip in range(1, 4)]
    tables = [table_grad] + [along_quad(table_grad, size, flip) for flip in range(1, 4)]
    grad_tokens = token_grad(late_grads, qkv_parts, tokens, gain_first[None], grad_res)
    arrived, tables, grad_tokens, by_flip = lax.optimization_barrier(
        (arrived, tables, grad_tokens, by_flip)
    )
    table_grad = sum_all(tables)
    total = jnp.concatenate(
        [total, view[0] + sum(piece.astype(F32) for piece in arrived)], axis=1
    )
    sums = add_z(total, size)
    table_sum = sum_all(
        [table_grad] + [along_z_flip(table_grad, size, flip) for flip in range(1, depth)]
    )
    table_sum = table_sum.reshape(HEADS, BUCKETS).T
    out_sum = sums[:, :D]
    router_sum = sums[:, D : D + EXPERTS]
    gain_second_sum = sums[:, D + EXPERTS]
    qkv_sum = (
        sums[:, D + 128 :]
        .reshape(owned, PARTS, 3, PART)
        .transpose(0, 2, 1, 3)
        .reshape(owned, 3 * D)
    )

    gain_first_sum = jnp.sum(w_qkv.astype(F32) * qkv_sum, axis=1) / gain_attn.astype(F32)

    by_flip = jnp.stack(by_flip, axis=2).astype(F32)
    by_expert = jnp.concatenate(
        [lax.dynamic_slice_in_dim(by_flip, quad ^ expert, 1, 2) for expert in range(EXPERTS)],
        axis=2,
    )
    return (
        output,
        grad_tokens,
        gain_first_sum,
        qkv_sum,
        out_sum,
        table_sum,
        gain_second_sum,
        router_sum,
        by_expert[0],
        by_expert[1],
    )


def solution(mesh):
    rows = P(AXIS, None)
    in_specs = (
        rows, rows, rows, rows, P(AXIS), rows, rows, P(), P(AXIS), rows,
        P(AXIS, None, None), P(AXIS, None, None),
    )
    out_specs = (
        rows, rows, P(AXIS), rows, rows, P(), P(AXIS), rows,
        P(AXIS, None, None), P(AXIS, None, None),
    )
    return jax.shard_map(
        functools.partial(body, mesh.shape[AXIS]),
        mesh=mesh,
        in_specs=in_specs,
        out_specs=out_specs,
        check_vma=False,
    )
```

```python
import functools

import jax
import jax.numpy as jnp
from jax import lax
from jax.experimental import pallas as pl
from jax.experimental.pallas import tpu as pltpu
from jax.sharding import PartitionSpec as P

D = 768
HEADS = 12
HEAD_DIM = 64
PAIRS = HEADS // 2
PARTS = 3
PART_PAIRS = PAIRS // PARTS
PART = D // PARTS
BUCKETS = 32
EXPERTS = 4
TOK_DEV = 1024
CAP = 512
ROW_CHUNK = 256
ROWS = EXPERTS * CAP
AXIS = "fsdp"
F32 = jnp.float32
BF16 = jnp.bfloat16

norm_eps = 1e-06
masked_fill = -1e30
far_steps = (12, 16, 23, 32, 46, 64, 91)

TILE = 128
KEY_TILES = TOK_DEV // TILE
QUERY_BLOCK = 512
QUERY_BLOCKS = TOK_DEV // QUERY_BLOCK
HALVES = QUERY_BLOCK // TILE
NT = (((1,), (1,)), ((), ()))
NN = (((1,), (0,)), ((), ()))
TN = (((0,), (0,)), ((), ()))


def bucket_of(offset):
    distance = jnp.abs(offset)
    far_bucket = 8 + sum(((distance >= step).astype(jnp.int32) for step in far_steps))
    return jnp.where(distance < 8, distance, far_bucket) + 16 * (offset > 0).astype(jnp.int32)


def rms_norm(values, gain):
    return values * lax.rsqrt(jnp.mean(values * values, axis=-1, keepdims=True) + norm_eps) * gain


def along_z(value, size, shift):
    depth = size // 8
    return lax.ppermute(
        value, AXIS, [(i, (i // 8 + shift) % depth * 8 + i % 8) for i in range(size)]
    )


def along_quad(value, size, flip):
    return lax.ppermute(value, AXIS, [(i, i ^ (flip << 1)) for i in range(size)])


def along_core(value, size):
    return lax.ppermute(value, AXIS, [(i, i ^ 1) for i in range(size)])


def destinations(size, owned):
    me = lax.axis_index(AXIS)
    depth = size // 8
    z, quad, core = me // 8, me // 2 % 4, me % 2
    place = lax.iota(jnp.int32, size * owned)
    block, inner = place // owned, place % owned
    shift, flip, cross = block % depth, block // depth % 4, block // (depth * 4)
    owner = ((z + shift) % depth * 4 + (quad ^ flip)) * 2 + (core ^ cross)
    source = owner * owned + inner
    return (place[:, None] == source[None, :]).astype(BF16)


def for_quad(total):
    view = total.reshape(4, -1, total.shape[1])
    return [view[flip].astype(BF16) for flip in range(1, 4)], view


def sum_all(values):
    while len(values) > 1:
        half = len(values) // 2
        values = [left + right for left, right in zip(values[:half], values[half:])]
    return values[0]


def with_table(low, table):
    rows = low.shape[0]
    return jnp.concatenate([low, jnp.pad(table, ((0, rows - 3), (0, 0)))], axis=1)


def score_tile(tile, block, keys, queries, near_ref, head):
    scores = lax.dot_general(
        keys[tile * TILE : (tile + 1) * TILE], queries, NT, preferred_element_type=F32
    )
    parts = []
    for half in range(HALVES):
        part = scores[:, half * TILE : (half + 1) * TILE]
        apart = tile - (block * HALVES + half)
        if abs(apart) <= 1:
            part = part + near_ref[head, apart + 1]
        parts.append(part)
    return parts


def fold(value, combine):
    return combine(value.reshape(value.shape[0] // 8, 8, value.shape[1]), axis=0)


def attend_kernel(
    q_ref, k_ref, v_ref, extra_q_ref, extra_k_ref, near_ref, out_ref, log_ref,
    score_ref, prob_ref, turned_ref,
):
    lane = lax.broadcasted_iota(jnp.int32, (TOK_DEV, 2 * HEAD_DIM), 1)
    queries = (q_ref[...].astype(F32) * 0.125).astype(BF16)
    keys = k_ref[...]
    values_t = v_ref[...].astype(F32).T.astype(BF16)
    for head in range(2):
        own = (lane < HEAD_DIM) if head == 0 else (lane >= HEAD_DIM)
        head_keys = jnp.where(own, keys, extra_k_ref[head])
        head_queries = jnp.where(own, queries, extra_q_ref[head])
        head_values = values_t[head * HEAD_DIM : (head + 1) * HEAD_DIM]
        for block in range(QUERY_BLOCKS):
            side = block % 2
            at = slice(block * QUERY_BLOCK, (block + 1) * QUERY_BLOCK)
            top = None
            for tile in range(KEY_TILES):
                parts = score_tile(tile, block, head_keys, head_queries[at], near_ref, head)
                highs = []
                for half, part in enumerate(parts):
                    score_ref[
                        side, tile * TILE : (tile + 1) * TILE, half * TILE : (half + 1) * TILE
                    ] = part
                    highs.append(fold(part, jnp.max))
                high = jnp.concatenate(highs, axis=1)
                top = high if top is None else jnp.maximum(top, high)
            top = jnp.max(top, axis=0, keepdims=True)
            total = jnp.zeros((8, QUERY_BLOCK), F32)
            for tile in range(KEY_TILES):
                rows = slice(tile * TILE, (tile + 1) * TILE)
                expo = jnp.exp(score_ref[side, rows, :] - top)
                total = total + fold(expo, jnp.sum)
                prob_ref[side, rows, :] = expo.astype(BF16)
            total = jnp.sum(total, axis=0, keepdims=True)
            mixed = lax.dot_general(head_values, prob_ref[side], NN, preferred_element_type=F32)
            turned_ref[head * HEAD_DIM : (head + 1) * HEAD_DIM, at] = mixed * (1.0 / total)
            log_ref[0, head : head + 1, at] = top + jnp.log(total)
    out_ref[...] = turned_ref[...].T.astype(BF16)


def attend_back_kernel(
    q_ref, k_ref, v_ref, grad_ref, log_ref, extra_q_ref, extra_k_ref, near_ref, bucket_ref,
    grad_qkv_ref, grad_table_ref,
    prob_ref, slope_ref, low_prob_ref, low_grad_ref, turned_ref, key_sum_ref, value_sum_ref,
    near_sum_ref,
):
    lane = lax.broadcasted_iota(jnp.int32, (TOK_DEV, 2 * HEAD_DIM), 1)
    queries = (q_ref[...].astype(F32) * 0.125).astype(BF16)
    keys = k_ref[...]
    keys_t = (keys.astype(F32) * 0.125).T.astype(BF16)
    values = v_ref[...]
    grads = grad_ref[...]
    zero = jnp.zeros_like(grads)
    for head in range(2):
        own = (lane < HEAD_DIM) if head == 0 else (lane >= HEAD_DIM)
        head_keys = jnp.where(own, keys, extra_k_ref[head])
        head_queries = jnp.where(own, queries, extra_q_ref[head])
        bare_queries = jnp.where(own, queries, zero)
        head_grads = jnp.where(own, grads, zero)
        head_keys_t = keys_t[head * HEAD_DIM : (head + 1) * HEAD_DIM]
        near_sum_ref[...] = jnp.zeros_like(near_sum_ref)
        far_sums = [jnp.zeros((8, TILE), F32), jnp.zeros((8, TILE), F32)]
        for block in range(QUERY_BLOCKS):
            side = block % 2
            at = slice(block * QUERY_BLOCK, (block + 1) * QUERY_BLOCK)
            logs = log_ref[0, head : head + 1, at]
            delta = jnp.zeros((8, QUERY_BLOCK), F32)
            for tile in range(KEY_TILES):
                rows = slice(tile * TILE, (tile + 1) * TILE)
                parts = score_tile(tile, block, head_keys, head_queries[at], near_ref, head)
                probs = jnp.exp(jnp.concatenate(parts, axis=1) - logs)
                slopes = lax.dot_general(
                    values[rows], head_grads[at], NT, preferred_element_type=F32
                )
                delta = delta + fold(probs * slopes, jnp.sum)
                prob_ref[side, rows, :] = probs
                low_prob_ref[side, rows, :] = probs.astype(BF16)
                slope_ref[side, rows, :] = slopes
            delta = jnp.sum(delta, axis=0, keepdims=True)
            for tile in range(KEY_TILES):
                rows = slice(tile * TILE, (tile + 1) * TILE)
                grad_scores = prob_ref[side, rows, :] * (slope_ref[side, rows, :] - delta)
                low_grad_ref[side, rows, :] = grad_scores.astype(BF16)
                for half in range(HALVES):
                    part = grad_scores[:, half * TILE : (half + 1) * TILE]
                    apart = tile - (block * HALVES + half)
                    if abs(apart) <= 1:
                        near_sum_ref[apart + 1] += part
                    else:
                        which = 0 if apart < 0 else 1
                        far_sums[which] = far_sums[which] + fold(part, jnp.sum)
            value_part = lax.dot_general(
                low_prob_ref[side], head_grads[at], NN, preferred_element_type=F32
            )
            key_part = lax.dot_general(
                low_grad_ref[side], bare_queries[at], NN, preferred_element_type=F32
            )
            if head == 0 and block == 0:
                value_sum_ref[...] = value_part
                key_sum_ref[...] = key_part
            else:
                value_sum_ref[...] += value_part
                key_sum_ref[...] += key_part
            turned_ref[head * HEAD_DIM : (head + 1) * HEAD_DIM, at] = lax.dot_general(
                head_keys_t, low_grad_ref[side], NN, preferred_element_type=F32
            )
        for bucket in range(BUCKETS):
            row = jnp.zeros((8, TILE), F32)
            for apart in (-1, 0, 1):
                if (apart < 0 and bucket >= 16) or (apart > 0 and bucket < 16):
                    continue
                picked = jnp.where(
                    bucket_ref[apart + 1] == bucket, near_sum_ref[apart + 1], 0.0
                )
                row = row + fold(picked, jnp.sum)
            if bucket == 15:
                row = row + far_sums[0]
            if bucket == 31:
                row = row + far_sums[1]
            grad_table_ref[0, head, bucket : bucket + 1, :] = jnp.sum(row, axis=0, keepdims=True)
    grad_qkv_ref[0] = turned_ref[...].T.astype(BF16)
    grad_qkv_ref[1] = key_sum_ref[...].astype(BF16)
    grad_qkv_ref[2] = value_sum_ref[...].astype(BF16)


def column(first):
    return pl.BlockSpec((TOK_DEV, 2 * HEAD_DIM), lambda pair: (0, first + pair))


def score_specs(first):
    return [
        pl.BlockSpec((2, TOK_DEV, 2 * HEAD_DIM), lambda pair: (0, 0, 0)),
        pl.BlockSpec((2, TOK_DEV, 2 * HEAD_DIM), lambda pair: (first + pair, 0, 0)),
        pl.BlockSpec((2, 3, TILE, TILE), lambda pair: (first + pair, 0, 0, 0)),
    ]


def attend(qkv, extra_q, extra_k, near):
    logs = pl.BlockSpec((1, 2, TOK_DEV), lambda pair: (pair, 0, 0))
    return pl.pallas_call(
        attend_kernel,
        grid=(PAIRS,),
        in_specs=[column(0), column(PAIRS), column(2 * PAIRS)] + score_specs(0),
        out_specs=[column(0), logs],
        out_shape=[
            jax.ShapeDtypeStruct((TOK_DEV, D), BF16),
            jax.ShapeDtypeStruct((PAIRS, 2, TOK_DEV), F32),
        ],
        scratch_shapes=[
            pltpu.VMEM((2, TOK_DEV, QUERY_BLOCK), F32),
            pltpu.VMEM((2, TOK_DEV, QUERY_BLOCK), BF16),
            pltpu.VMEM((2 * HEAD_DIM, TOK_DEV), F32),
        ],
        compiler_params=pltpu.CompilerParams(vmem_limit_bytes=40 << 20),
        cost_estimate=pl.CostEstimate(
            flops=40_000_000_000, bytes_accessed=12 << 20, transcendentals=HEADS << 20
        ),
    )(qkv, qkv, qkv, extra_q, extra_k, near)


def attend_back(part, qkv, grad_mixed, logs, extra_q, extra_k, near, buckets):
    first = part * PART_PAIRS
    return pl.pallas_call(
        attend_back_kernel,
        grid=(PART_PAIRS,),
        in_specs=[
            column(first),
            column(PAIRS + first),
            column(2 * PAIRS + first),
            column(first),
            pl.BlockSpec((1, 2, TOK_DEV), lambda pair: (first + pair, 0, 0)),
        ]
        + score_specs(first)
        + [pl.BlockSpec((3, TILE, TILE), lambda pair: (0, 0, 0))],
        out_specs=[
            pl.BlockSpec((3, TOK_DEV, 2 * HEAD_DIM), lambda pair: (0, 0, pair)),
            pl.BlockSpec((1, 2, BUCKETS, TILE), lambda pair: (pair, 0, 0, 0)),
        ],
        out_shape=[
            jax.ShapeDtypeStruct((3, TOK_DEV, PART), BF16),
            jax.ShapeDtypeStruct((PART_PAIRS, 2, BUCKETS, TILE), F32),
        ],
        scratch_shapes=[
            pltpu.VMEM((2, TOK_DEV, QUERY_BLOCK), F32),
            pltpu.VMEM((2, TOK_DEV, QUERY_BLOCK), F32),
            pltpu.VMEM((2, TOK_DEV, QUERY_BLOCK), BF16),
            pltpu.VMEM((2, TOK_DEV, QUERY_BLOCK), BF16),
            pltpu.VMEM((2 * HEAD_DIM, TOK_DEV), F32),
            pltpu.VMEM((TOK_DEV, 2 * HEAD_DIM), F32),
            pltpu.VMEM((TOK_DEV, 2 * HEAD_DIM), F32),
            pltpu.VMEM((3, TILE, TILE), F32),
        ],
        compiler_params=pltpu.CompilerParams(vmem_limit_bytes=48 << 20),
        cost_estimate=pl.CostEstimate(
            flops=80_000_000_000 // PARTS,
            bytes_accessed=8 << 20,
            transcendentals=(HEADS << 20) // PARTS,
        ),
    )(qkv, qkv, qkv, grad_mixed, logs, extra_q, extra_k, near, buckets)


def score_extras(table, doc_ids):
    lane = lax.iota(jnp.int32, HEAD_DIM)
    places = lax.iota(jnp.int32, TOK_DEV)
    tiles = places // TILE
    is_doc = lane < 4
    block_lane = (lane >= 4) & (lane < 4 + KEY_TILES)
    same = doc_ids[:, None] == lane[None, :]
    in_block = tiles[:, None] == (lane - 4)[None, :]
    extra_q = jnp.where((is_doc & same) | (block_lane & in_block), 1.0, 0.0).astype(BF16)
    apart = tiles[:, None] - (lane - 4)[None, :]
    mask_k = jnp.where(is_doc & ~same, masked_fill, 0.0)
    far = jnp.where(
        apart[None] < 0, table[15].astype(F32)[:, None, None], table[31].astype(F32)[:, None, None]
    )
    use_far = (block_lane & (jnp.abs(apart) > 1))[None]
    extra_k = jnp.where(use_far, far, mask_k[None]).astype(BF16)
    blank = jnp.zeros_like(extra_q)
    queries = jnp.stack(
        [jnp.concatenate([blank, extra_q], axis=1), jnp.concatenate([extra_q, blank], axis=1)]
    )
    pairs = extra_k.reshape(PAIRS, 2, TOK_DEV, HEAD_DIM)
    even = jnp.concatenate([jnp.zeros_like(pairs[:, 0]), pairs[:, 0]], axis=-1)
    odd = jnp.concatenate([pairs[:, 1], jnp.zeros_like(pairs[:, 1])], axis=-1)
    keys = jnp.stack([even, odd], axis=1).reshape(HEADS, TOK_DEV, 2 * HEAD_DIM)
    return queries, keys


def gelu_with_slope(x):
    scale, cubic = 0.7978845608028654, 0.044715
    square = x * x
    half = 0.5 + 0.5 * jnp.tanh(x * (scale + (scale * cubic) * square))
    value = x * half
    slope = half + value * (1.0 - half) * (2.0 * scale + (6.0 * scale * cubic) * square)
    return value, slope


def expert_kernel(
    rows_ref, upstream_ref, gate_ref, up_ref, down_ref,
    out_ref, back_ref, grad_ref, hidden_ref, grad_pre_ref, out_sum_ref, back_sum_ref,
):
    step = pl.program_id(0)
    up = up_ref[...].reshape(-1, D)
    down = down_ref[...].reshape(-1, D)

    @pl.when(step == 0)
    def _():
        out_sum_ref[...] = jnp.zeros_like(out_sum_ref)
        back_sum_ref[...] = jnp.zeros_like(back_sum_ref)
        gate = jnp.broadcast_to(gate_ref[...], (TILE, CAP)).T
        for first in range(0, D, TILE):
            lanes = slice(first, first + TILE)
            grad_ref[:, lanes] = (gate * upstream_ref[:, lanes].astype(F32)).astype(BF16)

    for first in range(0, CAP, ROW_CHUNK):
        at = slice(first, first + ROW_CHUNK)
        pre = lax.dot_general(rows_ref[at], up, NT, preferred_element_type=F32)
        grad_hidden = lax.dot_general(grad_ref[at], down, NT, preferred_element_type=F32)
        hidden, slope = gelu_with_slope(pre)
        hidden = hidden.astype(BF16)
        grad_pre = (grad_hidden * slope).astype(BF16)
        hidden_ref[at] = hidden
        grad_pre_ref[at] = grad_pre
        out_sum_ref[at] += lax.dot_general(hidden, down, NN, preferred_element_type=F32)
        back_sum_ref[at] += lax.dot_general(grad_pre, up, NN, preferred_element_type=F32)

    @pl.when(step == pl.num_programs(0) - 1)
    def _():
        out_ref[...] = out_sum_ref[...].astype(BF16)
        back_ref[...] = back_sum_ref[...].astype(BF16)


def expert_weight_kernel(*refs):
    out_ref = refs[-1]
    rows, grads, hiddens, grad_pres = (refs[EXPERTS * i : EXPERTS * (i + 1)] for i in range(4))
    pieces, _, units, _ = out_ref.shape
    for which, lefts, rights in ((0, grad_pres, rows), (1, hiddens, grads)):
        total = None
        for left_ref, right_ref in zip(lefts, rights):
            part = lax.dot_general(
                left_ref[...], right_ref[...], TN, preferred_element_type=F32
            )
            total = part if total is None else total + part
        out_ref[:, which] = total.astype(BF16).reshape(pieces, units, D)


def weight_kernel(left_ref, right_ref, mine_ref, other_ref):
    half = D // 2
    for which in range(right_ref.shape[0]):
        width = right_ref.shape[2]
        lanes = slice(which * width, (which + 1) * width)
        for first, out_ref in ((0, mine_ref), (half, other_ref)):
            part = lax.dot_general(
                left_ref[:, first : first + half],
                right_ref[which],
                TN,
                preferred_element_type=F32,
            )
            out_ref[:, lanes] = part.astype(out_ref.dtype)


def weight_halves(left, right):
    width = right.shape[0] * right.shape[2]
    whole = pl.BlockSpec((TOK_DEV, D), lambda step: (0, 0))
    out = pl.BlockSpec((D // 2, width), lambda step: (0, 0))
    return pl.pallas_call(
        weight_kernel,
        grid=(1,),
        in_specs=[whole, pl.BlockSpec(right.shape, lambda step: (0, 0, 0))],
        out_specs=[out, out],
        out_shape=[
            jax.ShapeDtypeStruct((D // 2, width), F32),
            jax.ShapeDtypeStruct((D // 2, width), BF16),
        ],
        compiler_params=pltpu.CompilerParams(vmem_limit_bytes=40 << 20),
        cost_estimate=pl.CostEstimate(
            flops=2 * TOK_DEV * D * width, bytes_accessed=6 << 20, transcendentals=0
        ),
    )(left, right)


def token_grad_kernel(
    grads_0, grads_1, grads_2, weights_0, weights_1, weights_2, tokens_ref, gain_ref, rest_ref,
    out_ref,
):
    grad = None
    for grads_ref, weights_ref in zip(
        (grads_0, grads_1, grads_2), (weights_0, weights_1, weights_2)
    ):
        for which in range(3):
            part = lax.dot_general(
                grads_ref[which],
                weights_ref[:, which * PART : (which + 1) * PART],
                NT,
                preferred_element_type=F32,
            )
            grad = part if grad is None else grad + part
    values = tokens_ref[...].astype(F32)
    grad = grad * gain_ref[...]
    inverse = lax.rsqrt(jnp.mean(values * values, axis=-1, keepdims=True) + norm_eps)
    along = jnp.mean(values * grad, axis=-1, keepdims=True)
    out_ref[...] = (
        rest_ref[...] + inverse * (grad - values * (inverse * inverse * along))
    ).astype(BF16)


def token_grad(grads, weights, tokens, gain, rest):
    rows = TOK_DEV // 4
    part = pl.BlockSpec((rows, D), lambda step: (step, 0))
    return pl.pallas_call(
        token_grad_kernel,
        grid=(TOK_DEV // rows,),
        in_specs=[pl.BlockSpec((3, rows, PART), lambda step: (0, step, 0))] * PARTS
        + [pl.BlockSpec((D, 3 * PART), lambda step: (0, 0))] * PARTS
        + [part, pl.BlockSpec((1, D), lambda step: (0, 0)), part],
        out_specs=part,
        out_shape=jax.ShapeDtypeStruct((TOK_DEV, D), BF16),
        compiler_params=pltpu.CompilerParams(vmem_limit_bytes=48 << 20),
        cost_estimate=pl.CostEstimate(
            flops=6 * TOK_DEV * D * D, bytes_accessed=14 << 20, transcendentals=0
        ),
    )(*grads, *weights, tokens, gain, rest)


def early_kernel(
    slot_ref, values_ref, bucket_ref, table_ref, out_0, out_1, out_2, out_3, near_ref
):
    dispatch_kernel(slot_ref, values_ref, None, out_0, out_1, out_2, out_3)

    def fill(head, carry):
        for apart, first, last in ((0, 1, 16), (1, 0, BUCKETS), (2, 17, BUCKETS)):
            buckets = bucket_ref[apart]
            tile = jnp.zeros((TILE, TILE), F32)
            for bucket in range(first, last):
                tile = jnp.where(buckets == bucket, table_ref[bucket, head], tile)
            near_ref[head, apart] = tile
        return carry

    lax.fori_loop(0, HEADS, fill, 0)


def early(slot_row, values, buckets, table):
    vmem = pl.BlockSpec(memory_space=pltpu.VMEM)
    result = pl.pallas_call(
        early_kernel,
        in_specs=[vmem, vmem, vmem, pl.BlockSpec(memory_space=pltpu.SMEM)],
        out_shape=[jax.ShapeDtypeStruct((CAP, D), BF16)] * EXPERTS
        + [jax.ShapeDtypeStruct((HEADS, 3, TILE, TILE), F32)],
        compiler_params=pltpu.CompilerParams(vmem_limit_bytes=40 << 20),
        cost_estimate=pl.CostEstimate(
            flops=8 * ROWS * TOK_DEV * D, bytes_accessed=6 << 20, transcendentals=0
        ),
    )(slot_row, values, buckets, table)
    return list(result[:EXPERTS]), result[EXPERTS]


def dispatch_kernel(slot_ref, values_ref, gate_ref, out_0, out_1, out_2, out_3, *gate_outs):
    values = values_ref[...]
    for chunk, out_ref in enumerate((out_0, out_1, out_2, out_3)):
        wanted = chunk * CAP + lax.broadcasted_iota(jnp.int32, (CAP, TOK_DEV), 0)
        hit = wanted == slot_ref[...]
        out_ref[...] = lax.dot_general(
            jnp.where(hit, 1.0, 0.0).astype(BF16), values, NN, preferred_element_type=F32
        ).astype(BF16)
        if gate_outs:
            gates = jnp.sum(jnp.where(hit, gate_ref[...], 0.0), axis=1, keepdims=True)
            gate_outs[chunk][...] = jnp.broadcast_to(gates, (CAP, TILE)).T[0:1]


def dispatch(slot_row, values, gate_row):
    result = pl.pallas_call(
        dispatch_kernel,
        out_shape=[jax.ShapeDtypeStruct((CAP, D), BF16)] * EXPERTS
        + [jax.ShapeDtypeStruct((1, CAP), F32)] * EXPERTS,
        compiler_params=pltpu.CompilerParams(vmem_limit_bytes=40 << 20),
        cost_estimate=pl.CostEstimate(
            flops=2 * ROWS * TOK_DEV * D, bytes_accessed=6 << 20, transcendentals=0
        ),
    )(slot_row, values, gate_row)
    return list(result[:EXPERTS]), list(result[EXPERTS:])


def finish_kernel(
    slot_ref, attended_ref, upstream_ref, probs_ref, hot_ref, gate_ref, gain_ref, router_ref,
    weight_ref, *refs,
):
    pieces = refs[: 2 * EXPERTS]
    out_ref, rest_ref, low_ref, mixed_ref, logits_ref, gain_sum_ref = refs[2 * EXPERTS :]
    rows = slot_ref.shape[0]
    totals = [None, None]
    for chunk in range(EXPERTS):
        place = chunk * CAP + lax.broadcasted_iota(jnp.int32, (rows, CAP), 1)
        hit = jnp.where(place == slot_ref[...], 1.0, 0.0).astype(BF16)
        for which in range(2):
            part = lax.dot_general(
                hit, pieces[which * EXPERTS + chunk][...], NN, preferred_element_type=F32
            )
            totals[which] = part if totals[which] is None else totals[which] + part
    expert_rows, back_rows = totals
    attended, upstream = attended_ref[...], upstream_ref[...].astype(F32)
    gate = gate_ref[...]
    out_ref[...] = (attended + gate * expert_rows).astype(BF16)
    grad_gate = jnp.sum(upstream * expert_rows, axis=1, keepdims=True)
    grad_logits = probs_ref[...] * (grad_gate * hot_ref[...] - grad_gate * gate)
    logits_ref[...] = grad_logits
    grad_logits = grad_logits.astype(BF16).astype(F32)
    grad = back_rows
    for expert in range(EXPERTS):
        grad = grad + grad_logits[:, expert : expert + 1] * router_ref[expert : expert + 1]
    inverse = lax.rsqrt(jnp.mean(attended * attended, axis=-1, keepdims=True) + norm_eps)
    gain_part = jnp.sum(grad * (attended * inverse), axis=0, keepdims=True)

    @pl.when(pl.program_id(0) == 0)
    def _():
        gain_sum_ref[...] = gain_part

    @pl.when(pl.program_id(0) > 0)
    def _():
        gain_sum_ref[...] += gain_part

    grad = grad * gain_ref[...]
    along = jnp.mean(attended * grad, axis=-1, keepdims=True)
    rest = upstream + inverse * (grad - attended * (inverse * inverse * along))
    rest_ref[...] = rest
    low = rest.astype(BF16)
    low_ref[...] = low
    mixed_ref[...] = lax.dot_general(
        low, weight_ref[...], NT, preferred_element_type=F32
    ).astype(BF16)


def finish(slot_column, attended, upstream, probs, hot, gate, gain, router_t, weight, first, second):
    rows = TOK_DEV // 4

    def part(width):
        return pl.BlockSpec((rows, width), lambda step: (step, 0))

    def whole(shape):
        return pl.BlockSpec(shape, lambda step: (0, 0))

    return pl.pallas_call(
        finish_kernel,
        grid=(TOK_DEV // rows,),
        in_specs=[part(1), part(D), part(D), part(EXPERTS), part(EXPERTS), part(1)]
        + [whole((1, D)), whole((EXPERTS, D)), whole((D, D))]
        + [whole((CAP, D))] * (2 * EXPERTS),
        out_specs=[part(D), part(D), part(D), part(D), part(EXPERTS), whole((1, D))],
        out_shape=[
            jax.ShapeDtypeStruct((TOK_DEV, D), BF16),
            jax.ShapeDtypeStruct((TOK_DEV, D), F32),
            jax.ShapeDtypeStruct((TOK_DEV, D), BF16),
            jax.ShapeDtypeStruct((TOK_DEV, D), BF16),
            jax.ShapeDtypeStruct((TOK_DEV, EXPERTS), F32),
            jax.ShapeDtypeStruct((1, D), F32),
        ],
        compiler_params=pltpu.CompilerParams(vmem_limit_bytes=60 << 20),
        cost_estimate=pl.CostEstimate(
            flops=4 * ROWS * TOK_DEV * D, bytes_accessed=20 << 20, transcendentals=0
        ),
    )(
        slot_column, attended, upstream, probs, hot, gate, gain, router_t, weight,
        *first, *second,
    )


def expert_layout(weights, width):
    pieces, _, units, _ = weights.shape
    per_step = max(1, width // units)
    steps = pieces // per_step
    width = per_step * units
    whole = pl.BlockSpec((CAP, D), lambda step: (0, 0))
    part = pl.BlockSpec((CAP, width), lambda step: (0, step))
    up = pl.BlockSpec((per_step, 1, units, D), lambda step: (step, 0, 0, 0))
    down = pl.BlockSpec((per_step, 1, units, D), lambda step: (step, 1, 0, 0))
    both = pl.BlockSpec((per_step, 2, units, D), lambda step: (step, 0, 0, 0))
    return steps, steps * width, whole, part, up, down, both


def expert_pass(rows, upstream, gate, weights):
    steps, total, whole, part, up, down, _ = expert_layout(weights, D)
    return pl.pallas_call(
        expert_kernel,
        grid=(steps,),
        in_specs=[whole, whole, pl.BlockSpec((1, CAP), lambda step: (0, 0)), up, down],
        out_specs=[whole, whole, whole, part, part],
        out_shape=[jax.ShapeDtypeStruct((CAP, D), BF16)] * 3
        + [jax.ShapeDtypeStruct((CAP, total), BF16)] * 2,
        scratch_shapes=[pltpu.VMEM((CAP, D), F32)] * 2,
        compiler_params=pltpu.CompilerParams(vmem_limit_bytes=48 << 20),
        cost_estimate=pl.CostEstimate(
            flops=8 * CAP * D * total, bytes_accessed=20 << 20, transcendentals=CAP * total
        ),
    )(rows, upstream, gate, weights, weights)


def expert_weight_grads(rows, grads, hiddens, grad_pres, weights):
    steps, total, whole, part, _, _, both = expert_layout(weights, D // 2)
    return pl.pallas_call(
        expert_weight_kernel,
        grid=(steps,),
        in_specs=[whole] * (2 * EXPERTS) + [part] * (2 * EXPERTS),
        out_specs=both,
        out_shape=jax.ShapeDtypeStruct(weights.shape, BF16),
        compiler_params=pltpu.CompilerParams(vmem_limit_bytes=56 << 20),
        cost_estimate=pl.CostEstimate(
            flops=4 * ROWS * D * total, bytes_accessed=40 << 20, transcendentals=0
        ),
    )(*rows, *grads, *hiddens, *grad_pres)


def swap_rows(pieces, size):
    return [pieces[0]] + [along_quad(pieces[flip], size, flip) for flip in range(1, EXPERTS)]


def body(
    size,
    tokens,
    cotangent,
    lengths,
    routes,
    gain_attn,
    w_qkv,
    w_out,
    table,
    gain_ffn,
    router,
    expert_up,
    expert_down,
):
    quad = lax.axis_index(AXIS) // 2 % 4
    owned = w_qkv.shape[0]
    units = expert_up.shape[0]
    depth = size // 8
    same_expert = [
        [8 * z + 2 * q + c for z in range(depth) for c in range(2)] for q in range(EXPERTS)
    ]

    narrow = jnp.concatenate(
        [router, gain_attn[:, None], gain_ffn[:, None], jnp.zeros((owned, 128 - EXPERTS - 2), BF16)],
        axis=1,
    )
    owned_dense = jnp.concatenate([w_qkv, w_out, narrow], axis=1)
    z_dense = [along_z(owned_dense, size, -shift) for shift in range(1, depth)]
    hand_on = destinations(size, owned)
    turned_tokens = jnp.dot(tokens, hand_on, preferred_element_type=F32)

    def weights_for(flip):
        return jnp.stack(
            [
                lax.dynamic_index_in_dim(expert_up, quad ^ flip, 1, False),
                lax.dynamic_index_in_dim(expert_down, quad ^ flip, 1, False),
            ]
        )

    arrived_weights = swap_rows([weights_for(flip) for flip in range(EXPERTS)], size)
    ends = jnp.cumsum(lengths[0])
    places = lax.iota(jnp.int32, TOK_DEV)
    doc_ids = jnp.sum((places[:, None] >= ends[None, :]).astype(jnp.int32), axis=1)
    spread = lax.iota(jnp.int32, TILE)
    offsets = (
        TILE * jnp.arange(-1, 2)[:, None, None] + spread[None, :, None] - spread[None, None, :]
    )
    buckets = bucket_of(offsets)
    extra_q, extra_k = score_extras(table, doc_ids)

    route = routes[:, 0]
    chosen = (route[:, None] == lax.iota(jnp.int32, EXPERTS)[None, :]).astype(jnp.int32)
    rank = jnp.sum((jnp.cumsum(chosen, axis=0) - chosen) * chosen, axis=1)
    slot = (route ^ quad) * CAP + rank
    slot_row, slot_column = slot[None, :], slot[:, None]
    route_hot = chosen.astype(F32)

    tokens_f = tokens.astype(F32)
    (
        z_dense, arrived_weights, slot_row, buckets, extra_q, extra_k, turned_tokens, hand_on
    ) = lax.optimization_barrier(
        (
            z_dense, arrived_weights, slot_row, buckets, extra_q, extra_k, turned_tokens,
            hand_on,
        )
    )
    mine = jnp.stack(arrived_weights, axis=1)
    weights = lax.all_gather(
        mine.reshape(1, 2, EXPERTS * units, D),
        AXIS,
        axis=0,
        tiled=True,
        axis_index_groups=same_expert,
    )
    quad_dense = jnp.concatenate([owned_dense] + z_dense)
    arrived_dense = [along_quad(quad_dense, size, flip) for flip in range(1, 4)]
    (upstream_rows, near), arrived_dense = lax.optimization_barrier(
        (early(slot_row, cotangent, buckets, table.astype(F32)), arrived_dense)
    )
    core_dense = jnp.concatenate([quad_dense] + arrived_dense)
    dense = jnp.concatenate([core_dense, along_core(core_dense, size)])
    turned_gain = dense[:, 4 * D + EXPERTS].astype(F32)
    turned_normed = rms_norm(turned_tokens, turned_gain).astype(BF16)
    qkv = jnp.dot(turned_normed, dense[:, : 3 * D], preferred_element_type=F32).astype(BF16)
    upstream_rows, qkv = lax.optimization_barrier((upstream_rows, qkv))
    upstream_rows = swap_rows(upstream_rows, size)
    side = jnp.dot(hand_on, dense[:, 3 * D :], preferred_element_type=F32).astype(BF16)
    side, qkv = lax.optimization_barrier((side, qkv))
    out_w = side[:, :D]
    router_w = side[:, D : D + EXPERTS]
    gain_first = side[:, D + EXPERTS].astype(F32)
    gain_second = side[:, D + EXPERTS + 1].astype(F32)
    mixed, logs = attend(qkv, extra_q, extra_k, near)
    attended = tokens_f + jnp.dot(mixed, out_w, preferred_element_type=F32)
    normed_ffn = rms_norm(attended, gain_second).astype(BF16)
    logits = jnp.dot(normed_ffn, router_w, preferred_element_type=F32)
    probs_route = jax.nn.softmax(logits, axis=-1)
    gate = jnp.sum(probs_route * route_hot, axis=1, keepdims=True)
    normed_ffn, upstream_rows = lax.optimization_barrier((normed_ffn, upstream_rows))
    rows, gates = dispatch(slot_row, normed_ffn, gate.reshape(1, TOK_DEV))
    rows[0], late_mixed, late_dense = lax.optimization_barrier((rows[0], mixed, dense))
    gates = swap_rows(gates, size)
    rows[1], rows[2] = along_quad(rows[1], size, 1), along_quad(rows[2], size, 2)
    turned_mixed = jnp.dot(late_mixed, hand_on, preferred_element_type=F32).astype(BF16)
    qkv_parts = [
        jnp.dot(
            hand_on,
            jnp.concatenate(
                [
                    late_dense[:, which * D + part * PART : which * D + (part + 1) * PART]
                    for which in range(3)
                ],
                axis=1,
            ),
            preferred_element_type=F32,
        ).astype(BF16)
        for part in range(PARTS)
    ]
    router_t = router_w.astype(F32).T
    rows[1], rows[3], gates, turned_mixed, qkv_parts, router_t = lax.optimization_barrier(
        (rows[1], rows[3], gates, turned_mixed, qkv_parts, router_t)
    )
    rows[3] = along_quad(rows[3], size, 3)

    def run(flip, rows_in):
        return list(expert_pass(rows_in, upstream_rows[flip], gates[flip], weights))

    def out_of(flip, which):
        return along_quad(passes[flip][which], size, flip)

    passes = {}
    passes[1] = run(1, rows[1])
    rows_2, passes[1][2] = lax.optimization_barrier((rows[2], passes[1][2]))
    out_1 = out_of(1, 0)
    passes[2] = run(2, rows_2)
    passes[2][2], out_1 = lax.optimization_barrier((passes[2][2], out_1))
    rows_3, passes[2][2] = lax.optimization_barrier((rows[3], passes[2][2]))
    back_1, out_2 = out_of(1, 1), out_of(2, 0)
    passes[3] = run(3, rows_3)
    passes[3][2], back_1, out_2 = lax.optimization_barrier((passes[3][2], back_1, out_2))
    rows_0, passes[3][2] = lax.optimization_barrier((rows[0], passes[3][2]))
    back_2 = out_of(2, 1)
    passes[0] = run(0, rows_0)
    passes[0][2], back_2 = lax.optimization_barrier((passes[0][2], back_2))
    out_3, back_3 = out_of(3, 0), out_of(3, 1)
    order = [passes[flip] for flip in range(EXPERTS)]
    expert_grads = expert_weight_grads(
        rows, *([member[which] for member in order] for which in (2, 3, 4)), weights
    )
    expert_grads, out_3, back_3 = lax.optimization_barrier((expert_grads, out_3, back_3))
    output, grad_res, grad_attn_out, grad_mixed, grad_logits, grad_gain_second = finish(
        slot_column, attended, cotangent, probs_route, route_hot, gate, gain_second[None],
        router_t, out_w,
        (passes[0][0], out_1, out_2, out_3),
        (passes[0][1], back_1, back_2, back_3),
    )
    expert_sums = lax.psum_scatter(
        expert_grads, AXIS, scatter_dimension=0, tiled=True, axis_index_groups=same_expert
    ).reshape(2, EXPERTS, units, D)

    grad_logits = grad_logits.astype(BF16)
    grad_router = jnp.einsum("td,te->de", normed_ffn, grad_logits, preferred_element_type=F32)

    narrow = jnp.concatenate(
        [grad_router, grad_gain_second.T, jnp.zeros((D, 128 - EXPERTS - 1), F32)], axis=1
    ).astype(BF16)
    narrow = lax.dot_general(hand_on, narrow, TN, preferred_element_type=F32)
    narrow_mine, narrow_other = narrow[: D // 2], narrow[D // 2 :].astype(BF16)
    out_mine, out_other = weight_halves(turned_mixed, grad_attn_out[None])

    def attend_part(part, logs):
        return attend_back(part, qkv, grad_mixed, logs, extra_q, extra_k, near, buckets)

    grads_0, table_0 = attend_part(0, logs)
    mine, other = weight_halves(turned_normed, grads_0)
    other = jnp.concatenate([out_other, narrow_other, other], axis=1)
    mine = jnp.concatenate([out_mine, narrow_mine, mine], axis=1)
    logs, other, mine = lax.optimization_barrier((logs, other, mine))
    arrived = along_core(other, size)
    (grads_1, table_1), arrived = lax.optimization_barrier((attend_part(1, logs), arrived))
    low, view = for_quad(mine + arrived.astype(F32))
    mine_1, other_1 = weight_halves(turned_normed, grads_1)
    logs, low, view, other_1, mine_1 = lax.optimization_barrier(
        (logs, low, view, other_1, mine_1)
    )
    arrived_1 = along_core(other_1, size)
    arrived = [along_quad(low[flip - 1], size, flip) for flip in range(1, 4)]
    (grads_2, table_2), arrived, arrived_1, expert_sums = lax.optimization_barrier(
        (attend_part(2, logs), arrived, arrived_1, expert_sums)
    )
    mine_2, other_2 = weight_halves(turned_normed, grads_2)
    table_grad = jnp.concatenate(
        [
            jnp.sum(part, axis=-1).reshape(HEADS // PARTS, BUCKETS)
            for part in (table_0, table_1, table_2)
        ]
    ).reshape(-1, 128)
    by_flip = [expert_sums[:, flip] for flip in range(EXPERTS)]
    table_low = table_grad.astype(BF16)
    other_2, mine_2, table_low, by_flip = lax.optimization_barrier(
        (with_table(other_2, table_low), mine_2, table_low, by_flip)
    )

    arrived_2 = along_core(other_2, size)
    by_flip = swap_rows(by_flip, size)
    total = view[0] + sum(piece.astype(F32) for piece in arrived)
    late_1 = mine_1 + arrived_1.astype(F32)
    arrived_2, total, late_1, by_flip[1] = lax.optimization_barrier(
        (arrived_2, total, late_1, by_flip[1])
    )
    table_low = (table_low.astype(F32) + arrived_2[:3, 3 * PART :].astype(F32)).astype(BF16)
    low, view = for_quad(
        jnp.concatenate([late_1, mine_2 + arrived_2[:, : 3 * PART].astype(F32)], axis=1)
    )
    low = [with_table(piece, table_low) for piece in low]
    low, view, table_low, late_grads = lax.optimization_barrier(
        (low, view, table_low, [grads_0, grads_1, grads_2])
    )
    arrived = [along_quad(low[flip - 1], size, flip) for flip in range(1, 4)]
    grad_tokens = token_grad(late_grads, qkv_parts, tokens, gain_first[None], grad_res)
    arrived, grad_tokens, by_flip = lax.optimization_barrier((arrived, grad_tokens, by_flip))
    table_low = sum_all(
        [table_low.astype(F32)] + [piece[:3, 6 * PART :].astype(F32) for piece in arrived]
    ).astype(BF16)
    total = jnp.concatenate(
        [total, view[0] + sum(piece[:, : 6 * PART].astype(F32) for piece in arrived)], axis=1
    ).reshape(depth, owned, -1)
    width = total.shape[2]
    arrived = [
        along_z(with_table(total[shift].astype(BF16), table_low), size, shift)
        for shift in range(1, depth)
    ]
    sums = total[0] + sum(piece[:, :width].astype(F32) for piece in arrived)
    table_sum = sum_all(
        [table_low.astype(F32)] + [piece[:3, width:].astype(F32) for piece in arrived]
    )
    table_sum = table_sum.reshape(HEADS, BUCKETS).T
    out_sum = sums[:, :D]
    router_sum = sums[:, D : D + EXPERTS]
    gain_second_sum = sums[:, D + EXPERTS]
    qkv_sum = (
        sums[:, D + 128 :]
        .reshape(owned, PARTS, 3, PART)
        .transpose(0, 2, 1, 3)
        .reshape(owned, 3 * D)
    )

    gain_first_sum = jnp.sum(w_qkv.astype(F32) * qkv_sum, axis=1) / gain_attn.astype(F32)

    by_flip = jnp.stack(by_flip, axis=2).astype(F32)
    by_expert = jnp.concatenate(
        [lax.dynamic_slice_in_dim(by_flip, quad ^ expert, 1, 2) for expert in range(EXPERTS)],
        axis=2,
    )
    return (
        output,
        grad_tokens,
        gain_first_sum,
        qkv_sum,
        out_sum,
        table_sum,
        gain_second_sum,
        router_sum,
        by_expert[0],
        by_expert[1],
    )


def solution(mesh):
    rows = P(AXIS, None)
    in_specs = (
        rows, rows, rows, rows, P(AXIS), rows, rows, P(), P(AXIS), rows,
        P(AXIS, None, None), P(AXIS, None, None),
    )
    out_specs = (
        rows, rows, P(AXIS), rows, rows, P(), P(AXIS), rows,
        P(AXIS, None, None), P(AXIS, None, None),
    )
    return jax.shard_map(
        functools.partial(body, mesh.shape[AXIS]),
        mesh=mesh,
        in_specs=in_specs,
        out_specs=out_specs,
        check_vma=False,
    )
```

```python
import functools

import jax
import jax.numpy as jnp
from jax import lax
from jax.experimental import pallas as pl
from jax.experimental.pallas import tpu as pltpu
from jax.sharding import PartitionSpec as P

D = 768
HEADS = 12
HEAD_DIM = 64
PAIRS = HEADS // 2
PARTS = 3
PART_PAIRS = PAIRS // PARTS
PART = D // PARTS
BUCKETS = 32
EXPERTS = 4
TOK_DEV = 1024
CAP = 512
ROW_CHUNK = 256
ROWS = EXPERTS * CAP
AXIS = "fsdp"
F32 = jnp.float32
BF16 = jnp.bfloat16

norm_eps = 1e-06
masked_fill = -1e30
far_steps = (12, 16, 23, 32, 46, 64, 91)

TILE = 128
KEY_TILES = TOK_DEV // TILE
QUERY_BLOCK = 512
QUERY_BLOCKS = TOK_DEV // QUERY_BLOCK
HALVES = QUERY_BLOCK // TILE
NT = (((1,), (1,)), ((), ()))
NN = (((1,), (0,)), ((), ()))
TN = (((0,), (0,)), ((), ()))


def bucket_of(offset):
    distance = jnp.abs(offset)
    far_bucket = 8 + sum(((distance >= step).astype(jnp.int32) for step in far_steps))
    return jnp.where(distance < 8, distance, far_bucket) + 16 * (offset > 0).astype(jnp.int32)


def rms_norm(values, gain):
    return values * lax.rsqrt(jnp.mean(values * values, axis=-1, keepdims=True) + norm_eps) * gain


def along_z(value, size, shift):
    depth = size // 8
    return lax.ppermute(
        value, AXIS, [(i, (i // 8 + shift) % depth * 8 + i % 8) for i in range(size)]
    )


def along_quad(value, size, flip):
    return lax.ppermute(value, AXIS, [(i, i ^ (flip << 1)) for i in range(size)])


def along_core(value, size):
    return lax.ppermute(value, AXIS, [(i, i ^ 1) for i in range(size)])


def destinations(size, owned):
    me = lax.axis_index(AXIS)
    depth = size // 8
    z, quad, core = me // 8, me // 2 % 4, me % 2
    place = lax.iota(jnp.int32, size * owned)
    block, inner = place // owned, place % owned
    shift, flip, cross = block % depth, block // depth % 4, block // (depth * 4)
    owner = ((z + shift) % depth * 4 + (quad ^ flip)) * 2 + (core ^ cross)
    source = owner * owned + inner
    return (place[:, None] == source[None, :]).astype(BF16)


def for_quad(total):
    view = total.reshape(4, -1, total.shape[1])
    return [view[flip].astype(BF16) for flip in range(1, 4)], view


def sum_all(values):
    while len(values) > 1:
        half = len(values) // 2
        values = [left + right for left, right in zip(values[:half], values[half:])]
    return values[0]


def with_table(low, table):
    rows = low.shape[0]
    return jnp.concatenate([low, jnp.pad(table, ((0, rows - 3), (0, 0)))], axis=1)


def score_tile(tile, block, keys, queries, near_ref, head):
    scores = lax.dot_general(
        keys[tile * TILE : (tile + 1) * TILE], queries, NT, preferred_element_type=F32
    )
    parts = []
    for half in range(HALVES):
        part = scores[:, half * TILE : (half + 1) * TILE]
        apart = tile - (block * HALVES + half)
        if abs(apart) <= 1:
            part = part + near_ref[head, apart + 1]
        parts.append(part)
    return parts


def fold(value, combine):
    return combine(value.reshape(value.shape[0] // 8, 8, value.shape[1]), axis=0)


def attend_kernel(
    q_ref, k_ref, v_ref, extra_q_ref, extra_k_ref, near_ref, out_ref, log_ref,
    score_ref, prob_ref, turned_ref,
):
    lane = lax.broadcasted_iota(jnp.int32, (TOK_DEV, 2 * HEAD_DIM), 1)
    queries = (q_ref[...].astype(F32) * 0.125).astype(BF16)
    keys = k_ref[...]
    values_t = v_ref[...].astype(F32).T.astype(BF16)
    for head in range(2):
        own = (lane < HEAD_DIM) if head == 0 else (lane >= HEAD_DIM)
        head_keys = jnp.where(own, keys, extra_k_ref[head])
        head_queries = jnp.where(own, queries, extra_q_ref[head])
        head_values = values_t[head * HEAD_DIM : (head + 1) * HEAD_DIM]
        for block in range(QUERY_BLOCKS):
            side = block % 2
            at = slice(block * QUERY_BLOCK, (block + 1) * QUERY_BLOCK)
            top = None
            for tile in range(KEY_TILES):
                parts = score_tile(tile, block, head_keys, head_queries[at], near_ref, head)
                highs = []
                for half, part in enumerate(parts):
                    score_ref[
                        side, tile * TILE : (tile + 1) * TILE, half * TILE : (half + 1) * TILE
                    ] = part
                    highs.append(fold(part, jnp.max))
                high = jnp.concatenate(highs, axis=1)
                top = high if top is None else jnp.maximum(top, high)
            top = jnp.max(top, axis=0, keepdims=True)
            total = jnp.zeros((8, QUERY_BLOCK), F32)
            for tile in range(KEY_TILES):
                rows = slice(tile * TILE, (tile + 1) * TILE)
                expo = jnp.exp(score_ref[side, rows, :] - top)
                total = total + fold(expo, jnp.sum)
                prob_ref[side, rows, :] = expo.astype(BF16)
            total = jnp.sum(total, axis=0, keepdims=True)
            mixed = lax.dot_general(head_values, prob_ref[side], NN, preferred_element_type=F32)
            turned_ref[head * HEAD_DIM : (head + 1) * HEAD_DIM, at] = mixed * (1.0 / total)
            log_ref[0, head : head + 1, at] = top + jnp.log(total)
    out_ref[...] = turned_ref[...].T.astype(BF16)


def attend_back_kernel(
    q_ref, k_ref, v_ref, grad_ref, log_ref, extra_q_ref, extra_k_ref, near_ref, bucket_ref,
    grad_qkv_ref, grad_table_ref,
    prob_ref, slope_ref, low_prob_ref, low_grad_ref, turned_ref, key_sum_ref, value_sum_ref,
    near_sum_ref,
):
    lane = lax.broadcasted_iota(jnp.int32, (TOK_DEV, 2 * HEAD_DIM), 1)
    queries = (q_ref[...].astype(F32) * 0.125).astype(BF16)
    keys = k_ref[...]
    keys_t = (keys.astype(F32) * 0.125).T.astype(BF16)
    values = v_ref[...]
    grads = grad_ref[...]
    zero = jnp.zeros_like(grads)
    for head in range(2):
        own = (lane < HEAD_DIM) if head == 0 else (lane >= HEAD_DIM)
        head_keys = jnp.where(own, keys, extra_k_ref[head])
        head_queries = jnp.where(own, queries, extra_q_ref[head])
        bare_queries = jnp.where(own, queries, zero)
        head_grads = jnp.where(own, grads, zero)
        head_keys_t = keys_t[head * HEAD_DIM : (head + 1) * HEAD_DIM]
        near_sum_ref[...] = jnp.zeros_like(near_sum_ref)
        far_sums = [jnp.zeros((8, TILE), F32), jnp.zeros((8, TILE), F32)]
        for block in range(QUERY_BLOCKS):
            side = block % 2
            at = slice(block * QUERY_BLOCK, (block + 1) * QUERY_BLOCK)
            logs = log_ref[0, head : head + 1, at]
            delta = jnp.zeros((8, QUERY_BLOCK), F32)
            for tile in range(KEY_TILES):
                rows = slice(tile * TILE, (tile + 1) * TILE)
                parts = score_tile(tile, block, head_keys, head_queries[at], near_ref, head)
                probs = jnp.exp(jnp.concatenate(parts, axis=1) - logs)
                slopes = lax.dot_general(
                    values[rows], head_grads[at], NT, preferred_element_type=F32
                )
                delta = delta + fold(probs * slopes, jnp.sum)
                prob_ref[side, rows, :] = probs
                low_prob_ref[side, rows, :] = probs.astype(BF16)
                slope_ref[side, rows, :] = slopes
            delta = jnp.sum(delta, axis=0, keepdims=True)
            for tile in range(KEY_TILES):
                rows = slice(tile * TILE, (tile + 1) * TILE)
                grad_scores = prob_ref[side, rows, :] * (slope_ref[side, rows, :] - delta)
                low_grad_ref[side, rows, :] = grad_scores.astype(BF16)
                for half in range(HALVES):
                    part = grad_scores[:, half * TILE : (half + 1) * TILE]
                    apart = tile - (block * HALVES + half)
                    if abs(apart) <= 1:
                        near_sum_ref[apart + 1] += part
                    else:
                        which = 0 if apart < 0 else 1
                        far_sums[which] = far_sums[which] + fold(part, jnp.sum)
            value_part = lax.dot_general(
                low_prob_ref[side], head_grads[at], NN, preferred_element_type=F32
            )
            key_part = lax.dot_general(
                low_grad_ref[side], bare_queries[at], NN, preferred_element_type=F32
            )
            if head == 0 and block == 0:
                value_sum_ref[...] = value_part
                key_sum_ref[...] = key_part
            else:
                value_sum_ref[...] += value_part
                key_sum_ref[...] += key_part
            turned_ref[head * HEAD_DIM : (head + 1) * HEAD_DIM, at] = lax.dot_general(
                head_keys_t, low_grad_ref[side], NN, preferred_element_type=F32
            )
        for bucket in range(BUCKETS):
            row = jnp.zeros((8, TILE), F32)
            for apart in (-1, 0, 1):
                if (apart < 0 and bucket >= 16) or (apart > 0 and bucket < 16):
                    continue
                picked = jnp.where(
                    bucket_ref[apart + 1] == bucket, near_sum_ref[apart + 1], 0.0
                )
                row = row + fold(picked, jnp.sum)
            if bucket == 15:
                row = row + far_sums[0]
            if bucket == 31:
                row = row + far_sums[1]
            grad_table_ref[0, head, bucket : bucket + 1, :] = jnp.sum(row, axis=0, keepdims=True)
    grad_qkv_ref[0] = turned_ref[...].T.astype(BF16)
    grad_qkv_ref[1] = key_sum_ref[...].astype(BF16)
    grad_qkv_ref[2] = value_sum_ref[...].astype(BF16)


def column(first):
    return pl.BlockSpec((TOK_DEV, 2 * HEAD_DIM), lambda pair: (0, first + pair))


def score_specs(first):
    return [
        pl.BlockSpec((2, TOK_DEV, 2 * HEAD_DIM), lambda pair: (0, 0, 0)),
        pl.BlockSpec((2, TOK_DEV, 2 * HEAD_DIM), lambda pair: (first + pair, 0, 0)),
        pl.BlockSpec((2, 3, TILE, TILE), lambda pair: (first + pair, 0, 0, 0)),
    ]


def attend(qkv, extra_q, extra_k, near):
    logs = pl.BlockSpec((1, 2, TOK_DEV), lambda pair: (pair, 0, 0))
    return pl.pallas_call(
        attend_kernel,
        grid=(PAIRS,),
        in_specs=[column(0), column(PAIRS), column(2 * PAIRS)] + score_specs(0),
        out_specs=[column(0), logs],
        out_shape=[
            jax.ShapeDtypeStruct((TOK_DEV, D), BF16),
            jax.ShapeDtypeStruct((PAIRS, 2, TOK_DEV), F32),
        ],
        scratch_shapes=[
            pltpu.VMEM((2, TOK_DEV, QUERY_BLOCK), F32),
            pltpu.VMEM((2, TOK_DEV, QUERY_BLOCK), BF16),
            pltpu.VMEM((2 * HEAD_DIM, TOK_DEV), F32),
        ],
        compiler_params=pltpu.CompilerParams(vmem_limit_bytes=40 << 20),
        cost_estimate=pl.CostEstimate(
            flops=40_000_000_000, bytes_accessed=12 << 20, transcendentals=HEADS << 20
        ),
    )(qkv, qkv, qkv, extra_q, extra_k, near)


def attend_back(part, qkv, grad_mixed, logs, extra_q, extra_k, near, buckets):
    first = part * PART_PAIRS
    return pl.pallas_call(
        attend_back_kernel,
        grid=(PART_PAIRS,),
        in_specs=[
            column(first),
            column(PAIRS + first),
            column(2 * PAIRS + first),
            column(first),
            pl.BlockSpec((1, 2, TOK_DEV), lambda pair: (first + pair, 0, 0)),
        ]
        + score_specs(first)
        + [pl.BlockSpec((3, TILE, TILE), lambda pair: (0, 0, 0))],
        out_specs=[
            pl.BlockSpec((3, TOK_DEV, 2 * HEAD_DIM), lambda pair: (0, 0, pair)),
            pl.BlockSpec((1, 2, BUCKETS, TILE), lambda pair: (pair, 0, 0, 0)),
        ],
        out_shape=[
            jax.ShapeDtypeStruct((3, TOK_DEV, PART), BF16),
            jax.ShapeDtypeStruct((PART_PAIRS, 2, BUCKETS, TILE), F32),
        ],
        scratch_shapes=[
            pltpu.VMEM((2, TOK_DEV, QUERY_BLOCK), F32),
            pltpu.VMEM((2, TOK_DEV, QUERY_BLOCK), F32),
            pltpu.VMEM((2, TOK_DEV, QUERY_BLOCK), BF16),
            pltpu.VMEM((2, TOK_DEV, QUERY_BLOCK), BF16),
            pltpu.VMEM((2 * HEAD_DIM, TOK_DEV), F32),
            pltpu.VMEM((TOK_DEV, 2 * HEAD_DIM), F32),
            pltpu.VMEM((TOK_DEV, 2 * HEAD_DIM), F32),
            pltpu.VMEM((3, TILE, TILE), F32),
        ],
        compiler_params=pltpu.CompilerParams(vmem_limit_bytes=48 << 20),
        cost_estimate=pl.CostEstimate(
            flops=80_000_000_000 // PARTS,
            bytes_accessed=8 << 20,
            transcendentals=(HEADS << 20) // PARTS,
        ),
    )(qkv, qkv, qkv, grad_mixed, logs, extra_q, extra_k, near, buckets)


def score_extras(table, doc_ids):
    lane = lax.iota(jnp.int32, HEAD_DIM)
    places = lax.iota(jnp.int32, TOK_DEV)
    tiles = places // TILE
    is_doc = lane < 4
    block_lane = (lane >= 4) & (lane < 4 + KEY_TILES)
    same = doc_ids[:, None] == lane[None, :]
    in_block = tiles[:, None] == (lane - 4)[None, :]
    extra_q = jnp.where((is_doc & same) | (block_lane & in_block), 1.0, 0.0).astype(BF16)
    apart = tiles[:, None] - (lane - 4)[None, :]
    mask_k = jnp.where(is_doc & ~same, masked_fill, 0.0)
    far = jnp.where(
        apart[None] < 0, table[15].astype(F32)[:, None, None], table[31].astype(F32)[:, None, None]
    )
    use_far = (block_lane & (jnp.abs(apart) > 1))[None]
    extra_k = jnp.where(use_far, far, mask_k[None]).astype(BF16)
    blank = jnp.zeros_like(extra_q)
    queries = jnp.stack(
        [jnp.concatenate([blank, extra_q], axis=1), jnp.concatenate([extra_q, blank], axis=1)]
    )
    pairs = extra_k.reshape(PAIRS, 2, TOK_DEV, HEAD_DIM)
    even = jnp.concatenate([jnp.zeros_like(pairs[:, 0]), pairs[:, 0]], axis=-1)
    odd = jnp.concatenate([pairs[:, 1], jnp.zeros_like(pairs[:, 1])], axis=-1)
    keys = jnp.stack([even, odd], axis=1).reshape(HEADS, TOK_DEV, 2 * HEAD_DIM)
    return queries, keys


def gelu_with_slope(x):
    scale, cubic = 0.7978845608028654, 0.044715
    square = x * x
    half = 0.5 + 0.5 * jnp.tanh(x * (scale + (scale * cubic) * square))
    value = x * half
    slope = half + value * (1.0 - half) * (2.0 * scale + (6.0 * scale * cubic) * square)
    return value, slope


def expert_kernel(
    rows_ref, upstream_ref, gate_ref, up_ref, down_ref,
    out_ref, back_ref, grad_ref, hidden_ref, grad_pre_ref, out_sum_ref, back_sum_ref,
):
    step = pl.program_id(0)
    up = up_ref[...].reshape(-1, D)
    down = down_ref[...].reshape(-1, D)

    @pl.when(step == 0)
    def _():
        out_sum_ref[...] = jnp.zeros_like(out_sum_ref)
        back_sum_ref[...] = jnp.zeros_like(back_sum_ref)
        gate = jnp.broadcast_to(gate_ref[...], (TILE, CAP)).T
        for first in range(0, D, TILE):
            lanes = slice(first, first + TILE)
            grad_ref[:, lanes] = (gate * upstream_ref[:, lanes].astype(F32)).astype(BF16)

    for first in range(0, CAP, ROW_CHUNK):
        at = slice(first, first + ROW_CHUNK)
        pre = lax.dot_general(rows_ref[at], up, NT, preferred_element_type=F32)
        grad_hidden = lax.dot_general(grad_ref[at], down, NT, preferred_element_type=F32)
        hidden, slope = gelu_with_slope(pre)
        hidden = hidden.astype(BF16)
        grad_pre = (grad_hidden * slope).astype(BF16)
        hidden_ref[at] = hidden
        grad_pre_ref[at] = grad_pre
        out_sum_ref[at] += lax.dot_general(hidden, down, NN, preferred_element_type=F32)
        back_sum_ref[at] += lax.dot_general(grad_pre, up, NN, preferred_element_type=F32)

    @pl.when(step == pl.num_programs(0) - 1)
    def _():
        out_ref[...] = out_sum_ref[...].astype(BF16)
        back_ref[...] = back_sum_ref[...].astype(BF16)


def expert_weight_kernel(*refs):
    out_ref = refs[-1]
    rows, grads, hiddens, grad_pres = (refs[EXPERTS * i : EXPERTS * (i + 1)] for i in range(4))
    pieces, _, units, _ = out_ref.shape
    for which, lefts, rights in ((0, grad_pres, rows), (1, hiddens, grads)):
        total = None
        for left_ref, right_ref in zip(lefts, rights):
            part = lax.dot_general(
                left_ref[...], right_ref[...], TN, preferred_element_type=F32
            )
            total = part if total is None else total + part
        out_ref[:, which] = total.astype(BF16).reshape(pieces, units, D)


def weight_kernel(left_ref, right_ref, mine_ref, other_ref):
    half = D // 2
    for which in range(right_ref.shape[0]):
        width = right_ref.shape[2]
        lanes = slice(which * width, (which + 1) * width)
        for first, out_ref in ((0, mine_ref), (half, other_ref)):
            part = lax.dot_general(
                left_ref[:, first : first + half],
                right_ref[which],
                TN,
                preferred_element_type=F32,
            )
            out_ref[:, lanes] = part.astype(out_ref.dtype)


def weight_halves(left, right):
    width = right.shape[0] * right.shape[2]
    whole = pl.BlockSpec((TOK_DEV, D), lambda step: (0, 0))
    out = pl.BlockSpec((D // 2, width), lambda step: (0, 0))
    return pl.pallas_call(
        weight_kernel,
        grid=(1,),
        in_specs=[whole, pl.BlockSpec(right.shape, lambda step: (0, 0, 0))],
        out_specs=[out, out],
        out_shape=[
            jax.ShapeDtypeStruct((D // 2, width), F32),
            jax.ShapeDtypeStruct((D // 2, width), BF16),
        ],
        compiler_params=pltpu.CompilerParams(vmem_limit_bytes=40 << 20),
        cost_estimate=pl.CostEstimate(
            flops=2 * TOK_DEV * D * width, bytes_accessed=6 << 20, transcendentals=0
        ),
    )(left, right)


def token_grad_kernel(
    grads_0, grads_1, grads_2, weights_0, weights_1, weights_2, tokens_ref, gain_ref, rest_ref,
    out_ref,
):
    grad = None
    for grads_ref, weights_ref in zip(
        (grads_0, grads_1, grads_2), (weights_0, weights_1, weights_2)
    ):
        for which in range(3):
            part = lax.dot_general(
                grads_ref[which],
                weights_ref[:, which * PART : (which + 1) * PART],
                NT,
                preferred_element_type=F32,
            )
            grad = part if grad is None else grad + part
    values = tokens_ref[...].astype(F32)
    grad = grad * gain_ref[...]
    inverse = lax.rsqrt(jnp.mean(values * values, axis=-1, keepdims=True) + norm_eps)
    along = jnp.mean(values * grad, axis=-1, keepdims=True)
    out_ref[...] = (
        rest_ref[...] + inverse * (grad - values * (inverse * inverse * along))
    ).astype(BF16)


def token_grad(grads, weights, tokens, gain, rest):
    rows = TOK_DEV // 4
    part = pl.BlockSpec((rows, D), lambda step: (step, 0))
    return pl.pallas_call(
        token_grad_kernel,
        grid=(TOK_DEV // rows,),
        in_specs=[pl.BlockSpec((3, rows, PART), lambda step: (0, step, 0))] * PARTS
        + [pl.BlockSpec((D, 3 * PART), lambda step: (0, 0))] * PARTS
        + [part, pl.BlockSpec((1, D), lambda step: (0, 0)), part],
        out_specs=part,
        out_shape=jax.ShapeDtypeStruct((TOK_DEV, D), BF16),
        compiler_params=pltpu.CompilerParams(vmem_limit_bytes=48 << 20),
        cost_estimate=pl.CostEstimate(
            flops=6 * TOK_DEV * D * D, bytes_accessed=14 << 20, transcendentals=0
        ),
    )(*grads, *weights, tokens, gain, rest)


def early_kernel(
    slot_ref, values_ref, bucket_ref, table_ref, out_0, out_1, out_2, out_3, near_ref
):
    dispatch_kernel(slot_ref, values_ref, None, out_0, out_1, out_2, out_3)

    def fill(head, carry):
        for apart, first, last in ((0, 1, 16), (1, 0, BUCKETS), (2, 17, BUCKETS)):
            buckets = bucket_ref[apart]
            tile = jnp.zeros((TILE, TILE), F32)
            for bucket in range(first, last):
                tile = jnp.where(buckets == bucket, table_ref[bucket, head], tile)
            near_ref[head, apart] = tile
        return carry

    lax.fori_loop(0, HEADS, fill, 0)


def early(slot_row, values, buckets, table):
    vmem = pl.BlockSpec(memory_space=pltpu.VMEM)
    result = pl.pallas_call(
        early_kernel,
        in_specs=[vmem, vmem, vmem, pl.BlockSpec(memory_space=pltpu.SMEM)],
        out_shape=[jax.ShapeDtypeStruct((CAP, D), BF16)] * EXPERTS
        + [jax.ShapeDtypeStruct((HEADS, 3, TILE, TILE), F32)],
        compiler_params=pltpu.CompilerParams(vmem_limit_bytes=40 << 20),
        cost_estimate=pl.CostEstimate(
            flops=8 * ROWS * TOK_DEV * D, bytes_accessed=6 << 20, transcendentals=0
        ),
    )(slot_row, values, buckets, table)
    return list(result[:EXPERTS]), result[EXPERTS]


def dispatch_kernel(slot_ref, values_ref, gate_ref, out_0, out_1, out_2, out_3, *gate_outs):
    values = values_ref[...]
    for chunk, out_ref in enumerate((out_0, out_1, out_2, out_3)):
        wanted = chunk * CAP + lax.broadcasted_iota(jnp.int32, (CAP, TOK_DEV), 0)
        hit = wanted == slot_ref[...]
        out_ref[...] = lax.dot_general(
            jnp.where(hit, 1.0, 0.0).astype(BF16), values, NN, preferred_element_type=F32
        ).astype(BF16)
        if gate_outs:
            gates = jnp.sum(jnp.where(hit, gate_ref[...], 0.0), axis=1, keepdims=True)
            gate_outs[chunk][...] = jnp.broadcast_to(gates, (CAP, TILE)).T[0:1]


def dispatch(slot_row, values, gate_row):
    result = pl.pallas_call(
        dispatch_kernel,
        out_shape=[jax.ShapeDtypeStruct((CAP, D), BF16)] * EXPERTS
        + [jax.ShapeDtypeStruct((1, CAP), F32)] * EXPERTS,
        compiler_params=pltpu.CompilerParams(vmem_limit_bytes=40 << 20),
        cost_estimate=pl.CostEstimate(
            flops=2 * ROWS * TOK_DEV * D, bytes_accessed=6 << 20, transcendentals=0
        ),
    )(slot_row, values, gate_row)
    return list(result[:EXPERTS]), list(result[EXPERTS:])


def finish_kernel(
    slot_ref, attended_ref, upstream_ref, probs_ref, hot_ref, narrow_ref, weight_ref, *refs,
):
    pieces = refs[: 2 * EXPERTS]
    out_ref, rest_ref, low_ref, mixed_ref, logits_ref, gain_sum_ref = refs[2 * EXPERTS :]
    rows = slot_ref.shape[0]
    totals = [None, None]
    for chunk in range(EXPERTS):
        place = chunk * CAP + lax.broadcasted_iota(jnp.int32, (rows, CAP), 1)
        hit = jnp.where(place == slot_ref[...], 1.0, 0.0).astype(BF16)
        for which in range(2):
            part = lax.dot_general(
                hit, pieces[which * EXPERTS + chunk][...], NN, preferred_element_type=F32
            )
            totals[which] = part if totals[which] is None else totals[which] + part
    expert_rows, back_rows = totals
    attended, upstream = attended_ref[...], upstream_ref[...].astype(F32)
    gate = jnp.sum(probs_ref[...] * hot_ref[...], axis=1, keepdims=True)
    narrow = narrow_ref[...].astype(F32)
    out_ref[...] = (attended + gate * expert_rows).astype(BF16)
    grad_gate = jnp.sum(upstream * expert_rows, axis=1, keepdims=True)
    grad_logits = probs_ref[...] * (grad_gate * hot_ref[...] - grad_gate * gate)
    logits_ref[...] = grad_logits
    grad_logits = grad_logits.astype(BF16).astype(F32)
    grad = back_rows
    for expert in range(EXPERTS):
        grad = grad + grad_logits[:, expert : expert + 1] * narrow[expert : expert + 1]
    inverse = lax.rsqrt(jnp.mean(attended * attended, axis=-1, keepdims=True) + norm_eps)
    gain_part = jnp.sum(grad * (attended * inverse), axis=0, keepdims=True)

    @pl.when(pl.program_id(0) == 0)
    def _():
        gain_sum_ref[...] = gain_part

    @pl.when(pl.program_id(0) > 0)
    def _():
        gain_sum_ref[...] += gain_part

    grad = grad * narrow[EXPERTS + 1 : EXPERTS + 2]
    along = jnp.mean(attended * grad, axis=-1, keepdims=True)
    rest = upstream + inverse * (grad - attended * (inverse * inverse * along))
    rest_ref[...] = rest
    low = rest.astype(BF16)
    low_ref[...] = low
    mixed_ref[...] = lax.dot_general(
        low, weight_ref[...], NT, preferred_element_type=F32
    ).astype(BF16)


def finish(slot_column, attended, upstream, probs, hot, narrow, weight, first, second):
    rows = TOK_DEV // 4

    def part(width):
        return pl.BlockSpec((rows, width), lambda step: (step, 0))

    def whole(shape):
        return pl.BlockSpec(shape, lambda step: (0, 0))

    return pl.pallas_call(
        finish_kernel,
        grid=(TOK_DEV // rows,),
        in_specs=[part(1), part(D), part(D), part(EXPERTS), part(EXPERTS)]
        + [whole((128, D)), whole((D, D))]
        + [whole((CAP, D))] * (2 * EXPERTS),
        out_specs=[part(D), part(D), part(D), part(D), part(EXPERTS), whole((1, D))],
        out_shape=[
            jax.ShapeDtypeStruct((TOK_DEV, D), BF16),
            jax.ShapeDtypeStruct((TOK_DEV, D), F32),
            jax.ShapeDtypeStruct((TOK_DEV, D), BF16),
            jax.ShapeDtypeStruct((TOK_DEV, D), BF16),
            jax.ShapeDtypeStruct((TOK_DEV, EXPERTS), F32),
            jax.ShapeDtypeStruct((1, D), F32),
        ],
        compiler_params=pltpu.CompilerParams(vmem_limit_bytes=60 << 20),
        cost_estimate=pl.CostEstimate(
            flops=4 * ROWS * TOK_DEV * D, bytes_accessed=20 << 20, transcendentals=0
        ),
    )(
        slot_column, attended, upstream, probs, hot, narrow, weight, *first, *second
    )


def expert_layout(weights, width):
    pieces, _, units, _ = weights.shape
    per_step = max(1, width // units)
    steps = pieces // per_step
    width = per_step * units
    whole = pl.BlockSpec((CAP, D), lambda step: (0, 0))
    part = pl.BlockSpec((CAP, width), lambda step: (0, step))
    up = pl.BlockSpec((per_step, 1, units, D), lambda step: (step, 0, 0, 0))
    down = pl.BlockSpec((per_step, 1, units, D), lambda step: (step, 1, 0, 0))
    both = pl.BlockSpec((per_step, 2, units, D), lambda step: (step, 0, 0, 0))
    return steps, steps * width, whole, part, up, down, both


def expert_pass(rows, upstream, gate, weights):
    steps, total, whole, part, up, down, _ = expert_layout(weights, D)
    return pl.pallas_call(
        expert_kernel,
        grid=(steps,),
        in_specs=[whole, whole, pl.BlockSpec((1, CAP), lambda step: (0, 0)), up, down],
        out_specs=[whole, whole, whole, part, part],
        out_shape=[jax.ShapeDtypeStruct((CAP, D), BF16)] * 3
        + [jax.ShapeDtypeStruct((CAP, total), BF16)] * 2,
        scratch_shapes=[pltpu.VMEM((CAP, D), F32)] * 2,
        compiler_params=pltpu.CompilerParams(vmem_limit_bytes=48 << 20),
        cost_estimate=pl.CostEstimate(
            flops=8 * CAP * D * total, bytes_accessed=20 << 20, transcendentals=CAP * total
        ),
    )(rows, upstream, gate, weights, weights)


def expert_weight_grads(rows, grads, hiddens, grad_pres, weights):
    steps, total, whole, part, _, _, both = expert_layout(weights, D // 2)
    return pl.pallas_call(
        expert_weight_kernel,
        grid=(steps,),
        in_specs=[whole] * (2 * EXPERTS) + [part] * (2 * EXPERTS),
        out_specs=both,
        out_shape=jax.ShapeDtypeStruct(weights.shape, BF16),
        compiler_params=pltpu.CompilerParams(vmem_limit_bytes=56 << 20),
        cost_estimate=pl.CostEstimate(
            flops=4 * ROWS * D * total, bytes_accessed=40 << 20, transcendentals=0
        ),
    )(*rows, *grads, *hiddens, *grad_pres)


def swap_rows(pieces, size):
    return [pieces[0]] + [along_quad(pieces[flip], size, flip) for flip in range(1, EXPERTS)]


def body(
    size,
    tokens,
    cotangent,
    lengths,
    routes,
    gain_attn,
    w_qkv,
    w_out,
    table,
    gain_ffn,
    router,
    expert_up,
    expert_down,
):
    quad = lax.axis_index(AXIS) // 2 % 4
    owned = w_qkv.shape[0]
    units = expert_up.shape[0]
    depth = size // 8
    same_expert = [
        [8 * z + 2 * q + c for z in range(depth) for c in range(2)] for q in range(EXPERTS)
    ]

    narrow = jnp.concatenate(
        [router, gain_attn[:, None], gain_ffn[:, None], jnp.zeros((owned, 128 - EXPERTS - 2), BF16)],
        axis=1,
    )
    owned_dense = jnp.concatenate([w_qkv, w_out, narrow], axis=1)
    z_dense = [along_z(owned_dense, size, -shift) for shift in range(1, depth)]
    hand_on = destinations(size, owned)
    turned_tokens = jnp.dot(tokens, hand_on, preferred_element_type=F32)

    def weights_for(flip):
        return jnp.stack(
            [
                lax.dynamic_index_in_dim(expert_up, quad ^ flip, 1, False),
                lax.dynamic_index_in_dim(expert_down, quad ^ flip, 1, False),
            ]
        )

    offered = [weights_for(flip) for flip in range(EXPERTS)]
    z_dense[0], offered[3] = lax.optimization_barrier((z_dense[0], offered[3]))
    arrived_weights = swap_rows(offered, size)
    ends = jnp.cumsum(lengths[0])
    places = lax.iota(jnp.int32, TOK_DEV)
    doc_ids = jnp.sum((places[:, None] >= ends[None, :]).astype(jnp.int32), axis=1)
    spread = lax.iota(jnp.int32, TILE)
    offsets = (
        TILE * jnp.arange(-1, 2)[:, None, None] + spread[None, :, None] - spread[None, None, :]
    )
    buckets = bucket_of(offsets)
    extra_q, extra_k = score_extras(table, doc_ids)

    route = routes[:, 0]
    chosen = (route[:, None] == lax.iota(jnp.int32, EXPERTS)[None, :]).astype(jnp.int32)
    rank = jnp.sum((jnp.cumsum(chosen, axis=0) - chosen) * chosen, axis=1)
    slot = (route ^ quad) * CAP + rank
    slot_row, slot_column = slot[None, :], slot[:, None]
    route_hot = chosen.astype(F32)

    tokens_f = tokens.astype(F32)
    (
        z_dense, arrived_weights, slot_row, buckets, extra_q, extra_k, turned_tokens, hand_on
    ) = lax.optimization_barrier(
        (
            z_dense, arrived_weights, slot_row, buckets, extra_q, extra_k, turned_tokens,
            hand_on,
        )
    )
    mine = jnp.stack(arrived_weights, axis=1)
    weights = lax.all_gather(
        mine.reshape(1, 2, EXPERTS * units, D),
        AXIS,
        axis=0,
        tiled=True,
        axis_index_groups=same_expert,
    )
    quad_dense = jnp.concatenate([owned_dense] + z_dense)
    arrived_dense = [along_quad(quad_dense, size, flip) for flip in range(1, 4)]
    (upstream_rows, near), arrived_dense = lax.optimization_barrier(
        (early(slot_row, cotangent, buckets, table.astype(F32)), arrived_dense)
    )
    core_dense = jnp.concatenate([quad_dense] + arrived_dense)
    dense = jnp.concatenate([core_dense, along_core(core_dense, size)])
    turned_gain = dense[:, 4 * D + EXPERTS].astype(F32)
    turned_normed = rms_norm(turned_tokens, turned_gain).astype(BF16)
    qkv = jnp.dot(turned_normed, dense[:, : 3 * D], preferred_element_type=F32).astype(BF16)
    upstream_rows, qkv = lax.optimization_barrier((upstream_rows, qkv))
    upstream_rows = swap_rows(upstream_rows, size)
    side = jnp.dot(hand_on, dense[:, 3 * D :], preferred_element_type=F32).astype(BF16)
    side, qkv = lax.optimization_barrier((side, qkv))
    out_w = side[:, :D]
    router_w = side[:, D : D + EXPERTS]
    gain_first = side[:, D + EXPERTS].astype(F32)
    gain_second = side[:, D + EXPERTS + 1].astype(F32)
    mixed, logs = attend(qkv, extra_q, extra_k, near)
    attended = tokens_f + jnp.dot(mixed, out_w, preferred_element_type=F32)
    normed_ffn = rms_norm(attended, gain_second).astype(BF16)
    logits = jnp.dot(normed_ffn, router_w, preferred_element_type=F32)
    probs_route = jax.nn.softmax(logits, axis=-1)
    gate = jnp.sum(probs_route * route_hot, axis=1, keepdims=True)
    normed_ffn, upstream_rows = lax.optimization_barrier((normed_ffn, upstream_rows))
    rows, gates = dispatch(slot_row, normed_ffn, gate.reshape(1, TOK_DEV))
    rows[0], late_mixed, late_dense = lax.optimization_barrier((rows[0], mixed, dense))
    gates = swap_rows(gates, size)
    rows[1], rows[2] = along_quad(rows[1], size, 1), along_quad(rows[2], size, 2)
    turned_mixed = jnp.dot(late_mixed, hand_on, preferred_element_type=F32).astype(BF16)
    qkv_parts = [
        jnp.dot(
            hand_on,
            jnp.concatenate(
                [
                    late_dense[:, which * D + part * PART : which * D + (part + 1) * PART]
                    for which in range(3)
                ],
                axis=1,
            ),
            preferred_element_type=F32,
        ).astype(BF16)
        for part in range(PARTS)
    ]
    narrow_t = lax.dot_general(
        late_dense[:, 4 * D :], hand_on, (((0,), (1,)), ((), ())), preferred_element_type=F32
    ).astype(BF16)
    rows[1], rows[3], gates, turned_mixed, qkv_parts, narrow_t, out_w_late = (
        lax.optimization_barrier(
            (rows[1], rows[3], gates, turned_mixed, qkv_parts, narrow_t, out_w)
        )
    )
    rows[3] = along_quad(rows[3], size, 3)

    def run(flip, rows_in):
        return list(expert_pass(rows_in, upstream_rows[flip], gates[flip], weights))

    def out_of(flip, which):
        return along_quad(passes[flip][which], size, flip)

    passes = {}
    passes[1] = run(1, rows[1])
    rows_2, passes[1][2] = lax.optimization_barrier((rows[2], passes[1][2]))
    out_1 = out_of(1, 0)
    passes[2] = run(2, rows_2)
    passes[2][2], out_1 = lax.optimization_barrier((passes[2][2], out_1))
    rows_3, passes[2][2] = lax.optimization_barrier((rows[3], passes[2][2]))
    back_1, out_2 = out_of(1, 1), out_of(2, 0)
    passes[3] = run(3, rows_3)
    passes[3][2], back_1, out_2 = lax.optimization_barrier((passes[3][2], back_1, out_2))
    rows_0, passes[3][2] = lax.optimization_barrier((rows[0], passes[3][2]))
    back_2 = out_of(2, 1)
    passes[0] = run(0, rows_0)
    passes[0][2], back_2 = lax.optimization_barrier((passes[0][2], back_2))
    out_3, back_3 = out_of(3, 0), out_of(3, 1)
    order = [passes[flip] for flip in range(EXPERTS)]
    expert_grads = expert_weight_grads(
        rows, *([member[which] for member in order] for which in (2, 3, 4)), weights
    )
    expert_grads, out_3, back_3 = lax.optimization_barrier((expert_grads, out_3, back_3))
    output, grad_res, grad_attn_out, grad_mixed, grad_logits, grad_gain_second = finish(
        slot_column, attended, cotangent, probs_route, route_hot, narrow_t, out_w_late,
        (passes[0][0], out_1, out_2, out_3),
        (passes[0][1], back_1, back_2, back_3),
    )
    expert_sums = lax.psum_scatter(
        expert_grads, AXIS, scatter_dimension=0, tiled=True, axis_index_groups=same_expert
    ).reshape(2, EXPERTS, units, D)

    grad_logits = grad_logits.astype(BF16)
    grad_router = jnp.einsum("td,te->de", normed_ffn, grad_logits, preferred_element_type=F32)

    narrow = jnp.concatenate(
        [grad_router, grad_gain_second.T, jnp.zeros((D, 128 - EXPERTS - 1), F32)], axis=1
    ).astype(BF16)
    narrow = lax.dot_general(hand_on, narrow, TN, preferred_element_type=F32)
    narrow_mine, narrow_other = narrow[: D // 2], narrow[D // 2 :].astype(BF16)
    out_mine, out_other = weight_halves(turned_mixed, grad_attn_out[None])

    def attend_part(part, logs):
        return attend_back(part, qkv, grad_mixed, logs, extra_q, extra_k, near, buckets)

    grads_0, table_0 = attend_part(0, logs)
    mine, other = weight_halves(turned_normed, grads_0)
    other = jnp.concatenate([out_other, narrow_other, other], axis=1)
    mine = jnp.concatenate([out_mine, narrow_mine, mine], axis=1)
    logs, other, mine = lax.optimization_barrier((logs, other, mine))
    arrived = along_core(other, size)
    (grads_1, table_1), arrived = lax.optimization_barrier((attend_part(1, logs), arrived))
    low, view = for_quad(mine + arrived.astype(F32))
    mine_1, other_1 = weight_halves(turned_normed, grads_1)
    logs, low, view, other_1, mine_1 = lax.optimization_barrier(
        (logs, low, view, other_1, mine_1)
    )
    arrived_1 = along_core(other_1, size)
    arrived = [along_quad(low[flip - 1], size, flip) for flip in range(1, 4)]
    (grads_2, table_2), arrived, arrived_1 = lax.optimization_barrier(
        (attend_part(2, logs), arrived, arrived_1)
    )
    mine_2, other_2 = weight_halves(turned_normed, grads_2)
    table_grad = jnp.concatenate(
        [
            jnp.sum(part, axis=-1).reshape(HEADS // PARTS, BUCKETS)
            for part in (table_0, table_1, table_2)
        ]
    ).reshape(-1, 128)
    table_low = table_grad.astype(BF16)
    other_2, mine_2, table_low, late_grads = lax.optimization_barrier(
        (with_table(other_2, table_low), mine_2, table_low, [grads_0, grads_1, grads_2])
    )

    arrived_2 = along_core(other_2, size)
    grad_tokens = token_grad(late_grads, qkv_parts, tokens, gain_first[None], grad_res)
    arrived_2, grad_tokens = lax.optimization_barrier((arrived_2, grad_tokens))
    total = view[0] + sum(piece.astype(F32) for piece in arrived)
    late_1 = mine_1 + arrived_1.astype(F32)
    table_low = (table_low.astype(F32) + arrived_2[:3, 3 * PART :].astype(F32)).astype(BF16)
    low, view = for_quad(
        jnp.concatenate([late_1, mine_2 + arrived_2[:, : 3 * PART].astype(F32)], axis=1)
    )
    low = [with_table(piece, table_low) for piece in low]
    by_flip = [expert_sums[:, flip] for flip in range(EXPERTS)]
    low, view, table_low, by_flip = lax.optimization_barrier((low, view, table_low, by_flip))
    arrived = [along_quad(low[flip - 1], size, flip) for flip in range(1, 4)]
    by_flip[1] = along_quad(by_flip[1], size, 1)
    arrived, by_flip = lax.optimization_barrier((arrived, by_flip))
    by_flip[2:] = [along_quad(by_flip[flip], size, flip) for flip in range(2, EXPERTS)]
    table_low = sum_all(
        [table_low.astype(F32)] + [piece[:3, 6 * PART :].astype(F32) for piece in arrived]
    ).astype(BF16)
    total = jnp.concatenate(
        [total, view[0] + sum(piece[:, : 6 * PART].astype(F32) for piece in arrived)], axis=1
    ).reshape(depth, owned, -1)
    width = total.shape[2]
    arrived = [
        along_z(with_table(total[shift].astype(BF16), table_low), size, shift)
        for shift in range(1, depth)
    ]
    sums = total[0] + sum(piece[:, :width].astype(F32) for piece in arrived)
    table_sum = sum_all(
        [table_low.astype(F32)] + [piece[:3, width:].astype(F32) for piece in arrived]
    )
    table_sum = table_sum.reshape(HEADS, BUCKETS).T
    out_sum = sums[:, :D]
    router_sum = sums[:, D : D + EXPERTS]
    gain_second_sum = sums[:, D + EXPERTS]
    qkv_sum = (
        sums[:, D + 128 :]
        .reshape(owned, PARTS, 3, PART)
        .transpose(0, 2, 1, 3)
        .reshape(owned, 3 * D)
    )

    gain_first_sum = jnp.sum(w_qkv.astype(F32) * qkv_sum, axis=1) / gain_attn.astype(F32)

    by_flip = jnp.stack(by_flip, axis=2).astype(F32)
    by_expert = jnp.concatenate(
        [lax.dynamic_slice_in_dim(by_flip, quad ^ expert, 1, 2) for expert in range(EXPERTS)],
        axis=2,
    )
    return (
        output,
        grad_tokens,
        gain_first_sum,
        qkv_sum,
        out_sum,
        table_sum,
        gain_second_sum,
        router_sum,
        by_expert[0],
        by_expert[1],
    )


def solution(mesh):
    rows = P(AXIS, None)
    in_specs = (
        rows, rows, rows, rows, P(AXIS), rows, rows, P(), P(AXIS), rows,
        P(AXIS, None, None), P(AXIS, None, None),
    )
    out_specs = (
        rows, rows, P(AXIS), rows, rows, P(), P(AXIS), rows,
        P(AXIS, None, None), P(AXIS, None, None),
    )
    return jax.shard_map(
        functools.partial(body, mesh.shape[AXIS]),
        mesh=mesh,
        in_specs=in_specs,
        out_specs=out_specs,
        check_vma=False,
    )
```
